32 devices in a mesh: groups: 2 (over x), leaf: 16 (over z, y, core).
Axes of the slice: x: 2, y: 2, z: 4, core: 2. Of those that a mesh axis runs over, the one named last changes fastest.
Arguments:
- points: float32 [256, 64, 256], P(('groups', 'leaf')), parts along dimension 0, may hold values from -6 to 6
- right_side: float32 [256, 256], P(('groups', 'leaf')), parts along dimension 0, may hold values from -6 to 6
- near_mask: int32 [256, 2], P(('groups', 'leaf')), parts along dimension 0, may hold values from 0 to 1, as said below
- far_dest: int32 [256, 4], P(('groups', 'leaf')), parts along dimension 0, may hold values from 0 to 15, all different within a row; in each aligned block of 8 rows (0 to 7, 8 to 15, ...) at most 4 rows name the same one
- far_leaf: int32 [256, 4], P(('groups', 'leaf')), parts along dimension 0, may hold values from 0 to 7
- skeleton: int32 [256, 128], P(('groups', 'leaf')), parts along dimension 0, may hold values from 0 to 255, as said below
- top_index: int32 [32, 128], P(('groups', 'leaf')), parts along dimension 0, may hold values from 0 to 2047, as said below
Outputs:
- solution_field: float32 [256, 256], P(('groups', 'leaf')), parts along dimension 0
- residual: float32 [256, 256], P(('groups', 'leaf')), parts along dimension 0
The draws below stay inside these ranges and needn't reach their ends.
There are 2 independent parts, one for each index of `groups`. The reference program is written for one: setup_inputs(seed, part) draws one part's arguments, and reference() takes and returns one part's arrays. A program takes and returns all parts, laid end to end along the dimension named above; each array names one. Nothing has to cross between parts.
Inputs may be any that keep to these rules, and one draw needn't show every extreme that they name: `near_mask`: each device's 8 rows hold at most 8 ones, and some device holds exactly 8. `skeleton`: entries within a row are distinct. `top_index`: entries within a row are distinct. `far_dest`: entries within a row are distinct; within the rows of one device no device number appears more than 4 times, and some number appears exactly 4 times.
All inputs are finite; a program needn't handle non-finite values.
Results may differ from the reference program's by a relative error of at most 0.0003.
Values sent between devices are 32-bit elements; how exact they have to be, the bound alone decides.
No kernel may reach another device: no remote copies, remote signals or barrier semaphores. Data moves between devices by JAX's collectives and lax.ppermute only.
A program may use at most 64 MiB of HBM per device.

```python
import math
import jax
import jax.numpy as jnp
import numpy as np
from jax import lax

DIM = 64
LEAF = 256
SKEL = 128
TOPR = 128
NF = 4
ITERS = 2
REACH = 2
LD = 8
NEAR_CAP = 8
FAR_CAP = 4
NL = 128
N_LEAF = 16


def draw_near_mask(key, part):
    key = jax.random.fold_in(key, 11)
    groups = NL // LD
    slots = LD * REACH
    count_key, force_key, order_key = jax.random.split(key, 3)
    shrink = jax.random.randint(count_key, (groups,), 0, 4)
    counts = jnp.maximum(1, NEAR_CAP // 2 ** shrink)
    forced = jax.random.randint(force_key, (), 0, groups)
    counts = jnp.where(jnp.arange(groups) == forced, NEAR_CAP, counts)
    orders = jax.vmap(lambda single: jax.random.permutation(single, slots))(jax.random.split(order_key, groups))
    active = (orders < counts[:, None]).astype(jnp.int32)
    return active.reshape(NL, REACH)


def draw_skeleton(key, part):
    key = jax.random.fold_in(key, 23)
    orders = jax.vmap(lambda single: jax.random.permutation(single, LEAF))(jax.random.split(key, NL))
    return orders[:, :SKEL].astype(jnp.int32)


def draw_top_index(key, part):
    key = jax.random.fold_in(key, 37)
    orders = jax.vmap(lambda single: jax.random.permutation(single, LD * LEAF))(jax.random.split(key, NL // LD))
    return orders[:, :TOPR].astype(jnp.int32)


def with_ends(entries, rng, smallest, top_value):
    spot = [jax.random.randint(jax.random.fold_in(rng, axis), (), 0, length) for axis, length in enumerate(entries.shape)]
    longest = entries.shape.index(max(entries.shape))
    neighbour = spot[:longest] + [(spot[longest] + 1) % entries.shape[longest]] + spot[longest + 1:]
    return entries.at[tuple(spot)].set(smallest).at[tuple(neighbour)].set(top_value)


def level_of(rng, shape, cuts, smallest, top_value):
    factor_of = 1.0
    for position, blocks in cuts:
        steps = jax.random.uniform(jax.random.fold_in(jax.random.fold_in(rng, 6), position), (blocks,), jnp.float32, smallest / len(cuts), top_value / len(cuts))
        factor_of = factor_of * jnp.repeat(jnp.exp(steps), shape[position] // blocks).reshape((-1,) + (1,) * (len(shape) - 1 - position))
    return factor_of


def assign_block(key, own, number, rows, number_of, top, most, skew):
    order = jax.random.permutation(key, number_of)
    heavy_load, ordinary = shares(number_of, rows * top, most, skew, True), shares(number_of, rows * top, most, skew, False)
    places = jnp.arange(number_of)

    def named(lengths, rotation):
        used = int((lengths > 0).sum())
        fixed = max(1, used // 4)
        passed = fixed + (places - fixed + rotation * (used - fixed)) % max(1, number_of - fixed)
        return jnp.zeros((number_of,), jnp.int32).at[order[jnp.where(places < fixed, places, passed)]].set(jnp.asarray(lengths, jnp.int32))

    lengths = jnp.where(number % 4 == 0, named(heavy_load, number // 4), named(ordinary, number - number // 4 - 1))
    mixed = jax.random.permutation(jax.random.fold_in(own, 3), number_of)
    giver, taker = mixed[0:number_of // 2 * 2:2], mixed[1:number_of // 2 * 2:2]
    slack = jnp.minimum(lengths[giver] - 1, most - lengths[taker]) // 2
    slack = jnp.where((giver == order[0]) | (taker == order[0]) | (lengths[taker] == 0), 0, jnp.maximum(slack, 0))
    passed = jax.random.randint(jax.random.fold_in(own, 4), (number_of // 2,), 0, 1 << 20) % (slack + 1)
    lengths = lengths.at[giver].add(-passed).at[taker].add(passed)
    items = jnp.searchsorted(jnp.cumsum(lengths), jnp.arange(rows * top), side="right").astype(jnp.int32)
    table = items.reshape(top, rows).T
    table = table[jax.random.permutation(jax.random.fold_in(own, 1), rows)]
    rotation = jax.random.randint(jax.random.fold_in(own, 2), (rows, 1), 0, top)
    return jnp.take_along_axis(table, (jnp.arange(top)[None, :] + rotation) % top, axis=1)


def shares(number_of, total, limit, skew, full):
    portions = [(1 << 20) // math.isqrt(grade ** skew) + 1 for grade in range(1, number_of + 1)]
    largest = limit if full else min(limit, max(-(-total // number_of), total * portions[0] // sum(portions)))
    least = 1 if total - largest >= number_of - 1 else 0
    holding, spare = [largest] + [least] * (number_of - 1), total - largest - least * (number_of - 1)
    while spare > 0:
        candidates = [i for i in range(1, number_of) if holding[i] < largest] or [i for i in range(1, number_of) if holding[i] < limit]
        mass, budget = sum([portions[i] for i in candidates]), spare
        for i in candidates:
            addition = min(limit - holding[i], max(1, budget * portions[i] // mass), spare)
            holding[i] = holding[i] + addition
            spare = spare - addition
    return np.array(holding)


def noise(stream_key, dims, deviation, bound, cuts=(), held_as=jnp.bfloat16):
    loudness = level_of(stream_key, dims, cuts, -0.22, 0.18) if cuts else 1.0
    array = jax.random.normal(stream_key, dims, jnp.float32) * deviation * loudness
    return jnp.minimum(jnp.maximum(array, -bound), bound).astype(held_as)


def setup_inputs(seed: int = 0, part: int = 0) -> dict:
    keys = jax.random.split(jax.random.key(seed), 8)
    own_keys = jax.random.split(jax.random.fold_in(keys[7], part), 8)
    points = noise(own_keys[0], (NL, DIM, LEAF), 1.0, 6.0, ((0, 16),), jnp.float32)
    right_side = noise(own_keys[1], (NL, LEAF), 1.0, 6.0, ((0, 16),), jnp.float32)
    near_mask = draw_near_mask(jax.random.fold_in(jax.random.fold_in(keys[7], part), 71), part)
    far_dest_keys = jax.random.split(jax.random.fold_in(own_keys[3], 1), NL // LD)
    far_dest_turns = jax.random.permutation(jax.random.fold_in(own_keys[3], 3), NL // LD)
    far_dest = jax.vmap(lambda own, number: assign_block(jax.random.fold_in(own_keys[3], 2), own, number, LD, N_LEAF, NF, FAR_CAP, 2))(far_dest_keys, far_dest_turns).reshape((NL, NF))
    far_leaf = with_ends(jax.random.randint(own_keys[4], (NL, NF), 0, LD), jax.random.fold_in(own_keys[4], 1), 0, LD - 1).astype(jnp.int32)
    skeleton = draw_skeleton(jax.random.fold_in(jax.random.fold_in(keys[7], part), 71), part)
    top_index = draw_top_index(jax.random.fold_in(jax.random.fold_in(keys[7], part), 71), part)
    return dict(points=points, right_side=right_side, near_mask=near_mask, far_dest=far_dest, far_leaf=far_leaf, skeleton=skeleton, top_index=top_index)


HIGHEST = lax.Precision.HIGHEST


def kernel_block(first_set, second_set):
    scale = 2.0 / first_set.shape[-2]
    cross_dots = jnp.einsum("...dm,...dn->...mn", first_set, second_set, precision=HIGHEST)
    first_sq = jnp.sum(first_set * first_set, axis=-2)
    second_sq = jnp.sum(second_set * second_set, axis=-2)
    distance = first_sq[..., :, None] + second_sq[..., None, :] - 2.0 * cross_dots
    return jnp.exp(-scale * distance)


def reference(points, right_side, near_mask, far_dest, far_leaf, skeleton, top_index):
    leaves_all = points.shape[0]
    reach = near_mask.shape[1]
    fan_out = far_dest.shape[1]
    device_count = leaves_all // LD
    leaf_ids = jnp.arange(leaves_all, dtype=jnp.int32)
    partner = (leaf_ids[:, None] + 1 + jnp.arange(reach, dtype=jnp.int32)[None, :]) % leaves_all
    mask_f = near_mask.astype(jnp.float32)
    far_partner = (far_dest * LD + far_leaf).astype(jnp.int32)
    skel_points = jnp.take_along_axis(points, jnp.broadcast_to(skeleton[:, None, :], (leaves_all, DIM, SKEL)), axis=2)
    dev_points = points.reshape(device_count, LD, DIM, LEAF).transpose(0, 2, 1, 3).reshape(device_count, DIM, LD * LEAF)
    tops = jnp.take_along_axis(dev_points, jnp.broadcast_to(top_index[:, None, :], (device_count, DIM, TOPR)), axis=2)
    all_tops = tops.transpose(1, 0, 2).reshape(DIM, device_count * TOPR)

    def apply(values):
        def near_leaf(index):
            own = points[index]
            others = points[partner[index]]
            tiles = kernel_block(jnp.broadcast_to(own, (reach, DIM, LEAF)), others)
            weights = mask_f[index]
            forward = jnp.einsum("rmn,rn,r->m", tiles, values[partner[index]], weights, precision=HIGHEST)
            backward = jnp.einsum("rmn,m->rn", tiles, values[index], precision=HIGHEST) * weights[:, None]
            diagonal = jnp.dot(kernel_block(own, own), values[index], precision=HIGHEST)
            return forward, backward, diagonal

        forward, backward, diagonal = lax.map(near_leaf, leaf_ids)
        near = forward + diagonal
        near = near.at[partner.reshape(-1)].add(backward.reshape(-1, LEAF))

        def leaf_coeffs(index):
            return jnp.dot(values[index], kernel_block(points[index], skel_points[index]), precision=HIGHEST)

        coeffs = lax.map(leaf_coeffs, leaf_ids)

        def far_entry(index):
            own = skel_points[index]
            tiles = kernel_block(jnp.broadcast_to(own, (fan_out, DIM, SKEL)), skel_points[far_partner[index]])
            to_own = jnp.einsum("fmn,fn->m", tiles, coeffs[far_partner[index]], precision=HIGHEST)
            to_other = jnp.einsum("fmn,m->fn", tiles, coeffs[index], precision=HIGHEST)
            self_term = jnp.dot(kernel_block(own, own), coeffs[index], precision=HIGHEST)
            return to_own, to_other, self_term

        to_own, to_other, self_term = lax.map(far_entry, leaf_ids)
        gathered = to_own + self_term
        gathered = gathered.at[far_partner.reshape(-1)].add(to_other.reshape(-1, SKEL))

        def far_expand(index):
            return jnp.dot(kernel_block(points[index], skel_points[index]), gathered[index], precision=HIGHEST)

        far = lax.map(far_expand, leaf_ids)
        dev_values = values.reshape(device_count, LD * LEAF)

        def coarse_of(pair):
            return jnp.dot(pair[2], kernel_block(pair[0], pair[1]), precision=HIGHEST)

        coarse = lax.map(coarse_of, (dev_points, tops, dev_values)).reshape(-1)

        def top_of(pair):
            mixed = jnp.dot(kernel_block(pair[1], all_tops), coarse, precision=HIGHEST)
            return jnp.dot(kernel_block(pair[0], pair[1]), mixed, precision=HIGHEST)

        top = lax.map(top_of, (dev_points, tops)).reshape(leaves_all, LEAF)
        return values + 0.25 * near + 0.125 * far + 0.25 * top

    solution_field = jnp.zeros_like(right_side)
    residual, direction = right_side, right_side
    norm_now = jnp.sum(residual * residual)
    for step in range(ITERS):
        image = apply(direction)
        alpha = norm_now / jnp.sum(direction * image)
        solution_field = solution_field + alpha * direction
        residual = residual - alpha * image
        norm_next = jnp.sum(residual * residual)
        direction = residual + (norm_next / norm_now) * direction
        norm_now = norm_next
    return solution_field, residual
```

```python
import functools
import math

import jax
import jax.numpy as jnp
from jax import lax
from jax.experimental import pallas as pl
from jax.experimental.pallas import tpu as pltpu
from jax.sharding import PartitionSpec as P

F32 = jnp.float32
BF16 = jnp.bfloat16
VMEM_LIMIT = 48 * 1024 * 1024
UNROLL = 4


def contract_first(left, right):
    return lax.dot_general(left, right, (((0,), (0,)), ((), ())), preferred_element_type=F32)


def halves(x):
    high = x.astype(BF16)
    return high, (x - high.astype(F32)).astype(BF16)


def thirds(x):
    high = x.astype(BF16)
    rest = x - high.astype(F32)
    middle = rest.astype(BF16)
    return high, middle, (rest - middle.astype(F32)).astype(BF16)


def norm_rows(x, factor, first):
    norm = jnp.sum(x * x, axis=0, keepdims=True) * factor
    high, middle, low = [piece.astype(F32) for piece in thirds(norm)]
    row = lax.broadcasted_iota(jnp.int32, (16, x.shape[1]), 0)
    rows = jnp.where(row < 6, 1.0, 0.0)
    for place, piece in ((first, high), (first + 1, middle), (first + 2, low)):
        rows = jnp.where(row == place, piece, rows)
    return rows.astype(BF16)


def unit(features):
    return 2.0 / features * math.log2(math.e)


def right_form(x):
    high, low = halves(x)
    return jnp.concatenate([high, high, low, norm_rows(x, -unit(x.shape[0]), 0)], axis=0)


def left_form(x):
    high, low = halves(x * (2.0 * unit(x.shape[0])))
    return jnp.concatenate([high, low, high, norm_rows(x, -unit(x.shape[0]), 3)], axis=0)


def tile_of(left, right):
    return jnp.exp2(contract_first(left, right))


def folded(tile, row):
    total = tile[:, :128] * row[:, :128]
    for start in range(128, tile.shape[1], 128):
        total = total + tile[:, start:start + 128] * row[:, start:start + 128]
    return total


def as_row(matrix):
    return jnp.sum(matrix.T, axis=0, keepdims=True)


def down(row):
    return jnp.broadcast_to(row, (128, row.shape[1])).T


def wide(column_matrix, columns):
    return jnp.concatenate([column_matrix] * (columns // 128), axis=1)


def prepare_kernel(points, values, mask, skeleton, top, piece, to_skel, to_top, lefts, first, last, rights):
    leaves, features, size = points.shape
    reach = first.shape[0]
    rank = skeleton.shape[1]
    pad = first.shape[1] - features - 1 - reach
    for r in range(reach):
        first[r, :features, :] = points[r]
        last[r, :features, :] = points[leaves - reach + r]
        first[r, features:, :] = jnp.broadcast_to(values[r:r + 1, :], (first.shape[1] - features, size))
        own = leaves - reach + r
        rows = [values[own:own + 1, :]]
        rows += [jnp.full((1, size), mask[own, s].astype(F32)) for s in range(reach)]
        last[r, features:, :] = jnp.concatenate(rows + [jnp.zeros((pad, size), F32)], axis=0)
    top_total = jnp.zeros((3 * features, rank), F32)
    spot = lax.broadcasted_iota(jnp.int32, (size, rank), 0)
    for l in range(leaves):
        x = points[l]
        chosen = jnp.concatenate(
            [spot == skeleton[l:l + 1, :], spot == top[...] - l * size], axis=1
        )
        picked = jnp.dot(
            jnp.concatenate(thirds(x), axis=0),
            jnp.where(chosen, 1.0, 0.0).astype(BF16),
            preferred_element_type=F32,
        )
        skel = picked[:, :rank]
        skel = skel[:features] + skel[features:2 * features] + skel[2 * features:]
        piece[l * features:(l + 1) * features, :] = skel
        lefts[l] = left_form(skel)
        rights[l] = right_form(x)
        top_total = top_total + picked[:, rank:]
    chosen_top = top_total[:features] + top_total[features:2 * features] + top_total[2 * features:]
    piece[leaves * features:(leaves + 1) * features, :] = chosen_top
    lefts[leaves] = left_form(chosen_top)
    coarse = jnp.zeros((rank, 128), F32)
    for l in range(leaves):
        both = tile_of(jnp.concatenate([lefts[l], lefts[leaves]], axis=1), rights[l])
        to_skel[l] = both[:rank]
        to_top[l] = both[rank:]
        row = values[l:l + 1, :]
        piece[(leaves + 1) * features + l:(leaves + 1) * features + l + 1, :] = as_row(
            folded(both[:rank], row)
        )
        coarse = coarse + folded(both[rank:], row)
    base = (leaves + 1) * features + leaves
    piece[base:base + 8, :] = jnp.broadcast_to(as_row(coarse), (8, rank))


def near_kernel(packed, points, values, mask, following, preceding, value_next, value_prev, out, lefts, rights, downs, across, along):
    leaves, features, size = points.shape
    reach = following.shape[0]

    def block(e):
        if e < reach:
            return preceding[e, :features, :]
        if e < reach + leaves:
            return points[e - reach]
        return following[e - reach - leaves, :features, :]

    def row_of(e):
        if reach <= e < reach + leaves:
            return values[e - reach:e - reach + 1, :]
        place = e if e < reach else e - reach - leaves
        if packed:
            return (preceding if e < reach else following)[place, features:features + 1, :]
        return (value_prev if e < reach else value_next)[place:place + 1, :]

    for e in range(leaves + 2 * reach):
        x = block(e)
        if e < leaves + reach:
            lefts[e] = left_form(x)
            downs[e] = down(row_of(e))
        if e >= reach:
            rights[e] = right_form(x)

    def backward(tile, a):
        product = tile * wide(downs[a], size)
        return jnp.sum(product.reshape(size // 8, 8, size), axis=0)

    for l in range(leaves):
        e = l + reach
        along[l] = backward(tile_of(lefts[e], rights[e]), e)
        across[l] = jnp.zeros((size, 128), F32)
    for a in range(leaves + reach):
        for r in range(reach):
            b = a + 1 + r
            own_a, own_b = reach <= a, reach <= b < reach + leaves
            if own_a:
                @pl.when(mask[a - reach, r] != 0)
                def _(a=a, b=b, own_b=own_b):
                    tile = tile_of(lefts[a], rights[b])
                    across[a - reach] += folded(tile, row_of(b))
                    if own_b:
                        along[b - reach] += backward(tile, a)
            elif own_b:
                weight = preceding[a, features + 1 + r:features + 2 + r, :]
                along[b - reach] += weight * backward(tile_of(lefts[a], rights[b]), a)
    for l in range(leaves):
        out[l:l + 1, :] = as_row(across[l]) + jnp.sum(along[l], axis=0, keepdims=True)


def make_list(axis, leaves, fan_out, dest, leaf, targets, sources, count):
    me = lax.axis_index(axis)
    mine = leaves * fan_out

    def clear(n, carry):
        targets[n] = leaves
        sources[n] = 0
        return carry

    lax.fori_loop(0, targets.shape[0], clear, 0)

    def own(n, carry):
        targets[n] = n // fan_out
        sources[n] = dest[me * mine + n] * leaves + leaf[me * mine + n]
        return carry

    lax.fori_loop(0, mine, own, 0)

    def itself(n, carry):
        targets[mine + n] = n
        sources[mine + n] = me * leaves + n
        return carry

    lax.fori_loop(0, leaves, itself, 0)

    def received(n, filled):
        here = dest[n] == me

        @pl.when(here)
        def _():
            targets[filled] = leaf[n]
            sources[filled] = n // fan_out

        return filled + here.astype(jnp.int32)

    count[0] = lax.fori_loop(0, dest.shape[0], received, mine + leaves)


def far_and_top(targets, sources, count, gathered, coefficients, lefts, to_skel, to_top, sums):
    leaves, rank, size = to_skel.shape
    features = (gathered.shape[1] - 16) // (leaves + 1)
    rows = coefficients.shape[1] - 16
    devices = gathered.shape[0]
    sums[...] = jnp.zeros_like(sums)

    def step(g, carry):
        found = []
        for k in range(UNROLL):
            n = g * UNROLL + k
            target, source = targets[n], sources[n]
            device, place = source // leaves, source % leaves
            start = pl.multiple_of(place * features, features)
            tile = tile_of(lefts[target], right_form(gathered[device, pl.ds(start, features), :]))
            found.append((target, tile * coefficients[device, pl.ds(rows + place, 1), :]))
        for target, product in found:
            sums[target] += product
        return carry

    lax.fori_loop(0, (count[0] + UNROLL - 1) // UNROLL, step, 0)

    def top_step(e, total):
        tile = tile_of(lefts[leaves], right_form(gathered[e, leaves * features:(leaves + 1) * features, :]))
        return total + tile * coefficients[e, rows + leaves:rows + leaves + 1, :]

    mixed = lax.fori_loop(0, devices, top_step, jnp.zeros((rank, rank), F32), unroll=4)
    mixed = jnp.sum(mixed, axis=1, keepdims=True)
    far, top = [], []
    for l in range(leaves):
        far.append(jnp.sum(to_skel[l] * jnp.sum(sums[l], axis=1, keepdims=True), axis=0, keepdims=True))
        top.append(jnp.sum(to_top[l] * mixed, axis=0, keepdims=True))
    return jnp.concatenate(far, axis=0), jnp.concatenate(top, axis=0)


def total_of(x):
    return jnp.sum(jnp.sum(x, axis=1, keepdims=True), axis=0, keepdims=True)


def in_lanes(*numbers):
    lane = lax.broadcasted_iota(jnp.int32, (1, 128), 1)
    row = jnp.zeros((1, 128), F32)
    for place, number in enumerate(numbers):
        row = jnp.where(lane == place, number, row)
    return row


def first_kernel(targets, sources, count, gathered, lefts, to_skel, to_top, values, near, image, head, tail, payload, sums):
    leaves, rank, size = to_skel.shape
    reach = head.shape[0]
    far, top = far_and_top(
        targets, sources, count, gathered, gathered, lefts, to_skel, to_top, sums
    )
    start = values[...]
    result = start + 0.25 * near[...] + 0.125 * far + 0.25 * top
    image[...] = result
    head[...] = result[:reach]
    tail[...] = result[leaves - reach:]
    coarse = jnp.zeros((rank, 128), F32)
    rows = []
    for l in range(leaves):
        row = result[l:l + 1, :]
        rows.append(as_row(folded(to_skel[l], row)))
        coarse = coarse + folded(to_top[l], row)
    rows.append(as_row(coarse))
    rows.append(in_lanes(total_of(start * start), total_of(start * result)))
    rows.append(jnp.zeros((16 - leaves - 2, 128), F32))
    payload[...] = jnp.concatenate(rows, axis=0)


def second_kernel(targets, sources, count, gathered, everyone, lefts, to_skel, to_top, values, image, near, residual, along, numbers, sums):
    leaves = to_skel.shape[0]
    far, top = far_and_top(
        targets, sources, count, gathered, everyone, lefts, to_skel, to_top, sums
    )
    start, first = values[...], image[...]
    second = first + 0.25 * near[...] + 0.125 * far + 0.25 * top
    scalars = jnp.sum(everyone[:, leaves + 1, :], axis=0, keepdims=True)
    norm, product = scalars[:, 0:1], scalars[:, 1:2]
    alpha = norm / product
    left = start - alpha * first
    image_left = first - alpha * second
    residual[...] = left
    along[...] = image_left
    row = in_lanes(total_of(left * left), total_of(left * image_left), norm, alpha)
    numbers[...] = jnp.broadcast_to(row, numbers.shape)


def last_kernel(everyone, numbers, values, image, residual, along, solution_field, final):
    scalars = jnp.sum(everyone[:, 0, :], axis=0, keepdims=True)
    norm_next, product = scalars[:, 0:1], scalars[:, 1:2]
    norm, alpha = numbers[0:1, 2:3], numbers[0:1, 3:4]
    ratio = norm_next / norm
    step = norm_next / (product - ratio * norm_next / alpha)
    start, left = values[...], residual[...]
    solution_field[...] = alpha * start + step * (left + ratio * start)
    final[...] = left - step * (along[...] + ratio * image[...])


def shape(*dims, dtype=F32):
    return jax.ShapeDtypeStruct(dims, dtype)


SMEM = pl.BlockSpec(memory_space=pltpu.SMEM)
VMEM = pl.BlockSpec(memory_space=pltpu.VMEM)


def kernel_call(body, name, inputs, outputs, scratch=()):
    out_specs, out_shapes = zip(*outputs)
    return pl.pallas_call(
        body,
        in_specs=list(inputs),
        out_specs=list(out_specs),
        out_shape=list(out_shapes),
        scratch_shapes=list(scratch),
        compiler_params=pltpu.CompilerParams(vmem_limit_bytes=VMEM_LIMIT),
        name=name,
    )


def passed_along(block, axis, distance):
    size = lax.axis_size(axis)
    return lax.ppermute(block, axis, [((i - distance) % size, i) for i in range(size)])


def everyones(block, axis):
    size = lax.axis_size(axis)
    return lax.all_to_all(
        jnp.broadcast_to(block[None], (size,) + block.shape), axis, split_axis=0, concat_axis=0, tiled=True
    )


def on_device(points, right_side, near_mask, far_dest, far_leaf, skeleton, top_index):
    leaves, features, size = points.shape
    reach = near_mask.shape[1]
    fan_out = far_dest.shape[1]
    rank = skeleton.shape[1]
    devices = lax.axis_size("leaf")
    capacity = max(2, (2 * leaves * fan_out + devices - 1) // devices)
    depth = 3 * features + 16
    piece_rows = (leaves + 1) * features + 16
    halo_rows = features + 8

    piece, to_skel, to_top, lefts, first, last = kernel_call(
        prepare_kernel,
        "prepare",
        [VMEM, VMEM, SMEM, VMEM, VMEM],
        [
            (VMEM, shape(piece_rows, rank)),
            (VMEM, shape(leaves, rank, size)),
            (VMEM, shape(leaves, rank, size)),
            (VMEM, shape(leaves + 1, depth, rank, dtype=BF16)),
            (VMEM, shape(reach, halo_rows, size)),
            (VMEM, shape(reach, halo_rows, size)),
        ],
        [pltpu.VMEM((leaves, depth, size), BF16)],
    )(points, right_side, near_mask, skeleton, top_index)

    gathered = lax.all_gather(piece[None], "leaf", axis=0, tiled=True)
    following = passed_along(first, "leaf", -1)
    preceding = passed_along(last, "leaf", 1)
    lists = everyones(jnp.stack([far_dest.reshape(-1), far_leaf.reshape(-1)]), "leaf")
    lists = lists.reshape(devices, 2, leaves * fan_out)

    most = leaves * fan_out + leaves + capacity * devices
    most = -(-most // UNROLL) * UNROLL
    targets, sources, count = kernel_call(
        functools.partial(make_list, "leaf", leaves, fan_out),
        "far_list",
        [SMEM, SMEM],
        [
            (SMEM, shape(most, dtype=jnp.int32)),
            (SMEM, shape(most, dtype=jnp.int32)),
            (SMEM, shape(1, dtype=jnp.int32)),
        ],
    )(lists[:, 0].reshape(-1), lists[:, 1].reshape(-1))

    def near_apply(packed, values, value_next, value_prev):
        return kernel_call(
            functools.partial(near_kernel, packed),
            "near_first" if packed else "near_second",
            [VMEM, VMEM, SMEM, VMEM, VMEM, VMEM, VMEM],
            [(VMEM, shape(leaves, size))],
            [
                pltpu.VMEM((leaves + reach, depth, size), BF16),
                pltpu.VMEM((leaves + 2 * reach, depth, size), BF16),
                pltpu.VMEM((leaves + reach, size, 128), F32),
                pltpu.VMEM((leaves, size, 128), F32),
                pltpu.VMEM((leaves, 8, size), F32),
            ],
        )(points, values, near_mask, following, preceding, value_next, value_prev)[0]

    near = near_apply(True, right_side, right_side[:reach], right_side[:reach])
    sums = pltpu.VMEM((leaves + 1, rank, rank), F32)
    image, head, tail, payload = kernel_call(
        first_kernel,
        "far_first",
        [SMEM, SMEM, SMEM, VMEM, VMEM, VMEM, VMEM, VMEM, VMEM],
        [
            (VMEM, shape(leaves, size)),
            (VMEM, shape(reach, size)),
            (VMEM, shape(reach, size)),
            (VMEM, shape(16, rank)),
        ],
        [sums],
    )(targets, sources, count, gathered, lefts, to_skel, to_top, right_side, near)

    value_next = passed_along(head, "leaf", -1)
    value_prev = passed_along(tail, "leaf", 1)
    everyone = everyones(payload, "leaf").reshape(devices, 16, rank)
    near = near_apply(False, image, value_next, value_prev)
    residual, along, numbers = kernel_call(
        second_kernel,
        "far_second",
        [SMEM, SMEM, SMEM] + [VMEM] * 8,
        [
            (VMEM, shape(leaves, size)),
            (VMEM, shape(leaves, size)),
            (VMEM, shape(8, 128)),
        ],
        [sums],
    )(targets, sources, count, gathered, everyone, lefts, to_skel, to_top, right_side, image, near)

    scalars = everyones(numbers, "leaf").reshape(devices, 8, 128)
    solution_field, final = kernel_call(
        last_kernel,
        "finish",
        [VMEM] * 6,
        [(VMEM, shape(leaves, size)), (VMEM, shape(leaves, size))],
    )(scalars, numbers, right_side, image, residual, along)
    return solution_field, final


def solution(mesh):
    rows = P(("groups", "leaf"), None)
    in_specs = (P(("groups", "leaf"), None, None),) + (rows,) * 6
    return jax.shard_map(
        on_device, mesh=mesh, in_specs=in_specs, out_specs=(rows, rows), check_vma=False
    )
```

```python
import functools
import math

import jax
import jax.numpy as jnp
from jax import lax
from jax.experimental import pallas as pl
from jax.experimental.pallas import tpu as pltpu
from jax.sharding import PartitionSpec as P

F32 = jnp.float32
BF16 = jnp.bfloat16
VMEM_LIMIT = 20 * 1024 * 1024
UNROLL = 4
GRID_DEVICES = 16
ORDER = ((0, 0), (0, 1), (1, 0), (3, 0), (1, 1), (3, 1), (2, 0), (2, 1))


def contract_first(left, right):
    return lax.dot_general(left, right, (((0,), (0,)), ((), ())), preferred_element_type=F32)


def halves(x):
    high = x.astype(BF16)
    return high, (x - high.astype(F32)).astype(BF16)


def thirds(x):
    high = x.astype(BF16)
    rest = x - high.astype(F32)
    middle = rest.astype(BF16)
    return high, middle, (rest - middle.astype(F32)).astype(BF16)


def norm_rows(x, factor, first):
    norm = jnp.sum(x * x, axis=0, keepdims=True) * factor
    high, middle, low = [piece.astype(F32) for piece in thirds(norm)]
    row = lax.broadcasted_iota(jnp.int32, (16, x.shape[1]), 0)
    rows = jnp.where(row < 6, 1.0, 0.0)
    for place, piece in ((first, high), (first + 1, middle), (first + 2, low)):
        rows = jnp.where(row == place, piece, rows)
    return rows.astype(BF16)


def unit(features):
    return 2.0 / features * math.log2(math.e)


def right_form(x):
    high, low = halves(x)
    return jnp.concatenate([high, high, low, norm_rows(x, -unit(x.shape[0]), 0)], axis=0)


def left_form(x):
    high, low = halves(x * (2.0 * unit(x.shape[0])))
    return jnp.concatenate([high, low, high, norm_rows(x, -unit(x.shape[0]), 3)], axis=0)


def tile_of(left, right):
    return jnp.exp2(contract_first(left, right))


def folded(tile, row):
    total = tile[:, :128] * row[:, :128]
    for start in range(128, tile.shape[1], 128):
        total = total + tile[:, start:start + 128] * row[:, start:start + 128]
    return total


def as_row(matrix):
    return jnp.sum(matrix.T, axis=0, keepdims=True)


def down(row):
    return jnp.broadcast_to(row, (128, row.shape[1])).T


def wide(column_matrix, columns):
    return jnp.concatenate([column_matrix] * (columns // 128), axis=1)


def owner_of(place, me, devices):
    if devices != GRID_DEVICES:
        return place
    turn, across = ORDER[place // 2]
    return (((me >> 2) - turn + 4) & 3) * 4 + ((me & 3) ^ (2 * across + place % 2))


def prepare_kernel(devices, capacity, *refs):
    (points_in, values_in, mask_in, skeleton_in, top_in, dest_in, leaf_in) = refs[:7]
    piece, again, to_skel, to_top, lefts, first, last = refs[7:14]
    points, values, mask, skeleton, top, dest, leaf, rights, sems = refs[14:]
    copies = []
    for n, (source, target) in enumerate(zip(refs[:7], (points, values, mask, skeleton, top, dest, leaf))):
        copies.append(pltpu.make_async_copy(source, target, sems.at[n]))
        copies[-1].start()
    for copy in copies:
        copy.wait()
    leaves, features, size = points.shape
    reach = first.shape[0]
    rank = skeleton.shape[1]
    fan_out = dest.shape[0]
    pad = first.shape[1] - features - 1 - reach
    top_total = jnp.zeros((3 * features, rank), F32)
    spot = lax.broadcasted_iota(jnp.int32, (size, rank), 0)
    for l in range(leaves):
        x = points[l]
        chosen = jnp.concatenate(
            [spot == skeleton[l:l + 1, :], spot == top[...] - l * size], axis=1
        )
        picked = jnp.dot(
            jnp.concatenate(thirds(x), axis=0),
            jnp.where(chosen, 1.0, 0.0).astype(BF16),
            preferred_element_type=F32,
        )
        skel = picked[:, :rank]
        skel = skel[:features] + skel[features:2 * features] + skel[2 * features:]
        piece[l * features:(l + 1) * features, :] = skel
        lefts[l] = left_form(skel)
        rights[l] = right_form(x)
        top_total = top_total + picked[:, rank:]
    chosen_top = top_total[:features] + top_total[features:2 * features] + top_total[2 * features:]
    piece[leaves * features:(leaves + 1) * features, :] = chosen_top
    lefts[leaves] = left_form(chosen_top)
    coarse = jnp.zeros((rank, 128), F32)
    base = (leaves + 1) * features
    for l in range(leaves):
        both = tile_of(jnp.concatenate([lefts[l], lefts[leaves]], axis=1), rights[l])
        to_skel[l] = both[:rank]
        to_top[l] = both[rank:]
        row = values[l:l + 1, :]
        piece[base + l:base + l + 1, :] = as_row(folded(both[:rank], row))
        coarse = coarse + folded(both[rank:], row)
    lane = lax.broadcasted_iota(jnp.int32, (1, 128), 1)
    codes = jnp.full((1, 128), -1.0, F32)
    seen = jnp.zeros((1, 128), jnp.int32)
    for l in range(leaves):
        for f in range(fan_out):
            here = lax.div(lane, jnp.int32(capacity)) == dest[f:f + 1, l:l + 1]
            code = (leaf[f:f + 1, l:l + 1] * leaves + l).astype(F32)
            codes = jnp.where(here & (lax.rem(lane, jnp.int32(capacity)) == seen), code, codes)
            seen = seen + here.astype(jnp.int32)
    piece[base + leaves:base + leaves + 8, :] = jnp.concatenate(
        [as_row(coarse), codes, jnp.zeros((6, 128), F32)], axis=0
    )
    again[...] = piece[...]
    for r in range(reach):
        first[r, :features, :] = points[r]
        last[r, :features, :] = points[leaves - reach + r]
        first[r, features:, :] = jnp.broadcast_to(values[r:r + 1, :], (first.shape[1] - features, size))
        own = leaves - reach + r
        rows = [values[own:own + 1, :]]
        rows += [jnp.broadcast_to(mask[s:s + 1, own:own + 1].astype(F32), (1, size)) for s in range(reach)]
        last[r, features:, :] = jnp.concatenate(rows + [jnp.zeros((pad, size), F32)], axis=0)


def edges_of(leaves, reach):
    pairs = [(a, r) for a in range(leaves + reach) for r in range(reach)]
    before = [(a, r) for a, r in pairs if a < reach <= a + 1 + r]
    after = [(a, r) for a, r in pairs if a >= reach and a + 1 + r >= leaves + reach]
    return before, after


def backward(tile, column):
    size = tile.shape[1]
    return jnp.sum((tile * wide(column, size)).reshape(-1, 8, size), axis=0)


def near_kernel(halo, points, values, mask, *refs):
    leaves, features, size = points.shape
    if halo:
        following, preceding, _, out, edges, _, lefts, rights, downs, across, along = refs
    else:
        out, lefts, rights, downs, across, along = refs
    reach = mask.shape[0]
    before, after = edges_of(leaves, reach)

    def block(e):
        if e < reach:
            return preceding[e, :features, :]
        if e < reach + leaves:
            return points[e - reach]
        return following[e - reach - leaves, :features, :]

    def row_of(e):
        if e < reach:
            return preceding[e, features:features + 1, :]
        if e < reach + leaves:
            return values[e - reach:e - reach + 1, :]
        return following[e - reach - leaves, features:features + 1, :]

    for e in range(leaves + 2 * reach):
        own = reach <= e < leaves + reach
        if own or halo:
            x = block(e)
            if e < leaves + reach:
                lefts[e] = left_form(x)
                downs[e] = down(row_of(e))
            if e >= reach:
                rights[e] = right_form(x)
    for l in range(leaves):
        e = l + reach
        along[l] = backward(tile_of(lefts[e], rights[e]), downs[e])
        across[l] = jnp.zeros((size, 128), F32)
    for a in range(leaves + reach):
        for r in range(reach):
            b = a + 1 + r
            if a >= reach and b < leaves + reach:
                @pl.when(mask[r, a - reach] != 0)
                def _(a=a, b=b):
                    tile = tile_of(lefts[a], rights[b])
                    across[a - reach] += folded(tile, row_of(b))
                    along[b - reach] += backward(tile, downs[a])
    if halo:
        for n, (a, r) in enumerate(before):
            b = a + 1 + r
            tile = tile_of(lefts[a], rights[b]) * preceding[a, features + 1 + r:features + 2 + r, :]
            edges[n] = tile
            along[b - reach] += backward(tile, downs[a])
        for n, (a, r) in enumerate(after):
            b = a + 1 + r
            place = len(before) + n

            @pl.when(mask[r, a - reach] == 0)
            def _(place=place):
                edges[place] = jnp.zeros((size, size), F32)

            @pl.when(mask[r, a - reach] != 0)
            def _(a=a, b=b, place=place):
                tile = tile_of(lefts[a], rights[b])
                edges[place] = tile
                across[a - reach] += folded(tile, row_of(b))

    for l in range(leaves):
        out[l:l + 1, :] = as_row(across[l]) + jnp.sum(along[l], axis=0, keepdims=True)


def far_group(axis, devices, capacity, places, own_piece, pieces, lefts, lists, tiles, tops, sums, scratch):
    targets, vectors, count = lists
    sources, rows, codes, sems = scratch
    leaves = lefts.shape[0] - 1
    features = (pieces[0].shape[0] - 16) // (leaves + 1)
    base = (leaves + 1) * features
    me = lax.axis_index(axis)
    copies = [
        pltpu.make_async_copy(ref.at[base + 8:base + 16, :], codes.at[n], sems.at[n])
        for n, ref in enumerate([own_piece] + list(pieces))
    ]
    for copy in copies:
        copy.start()
    for n, piece in enumerate(pieces):
        tile = tile_of(lefts[leaves], right_form(piece[leaves * features:(leaves + 1) * features, :]))
        tops[n] = tile
        sums[leaves + 1] += tile * piece[base + leaves:base + leaves + 1, :]
    for copy in copies:
        copy.wait()
    filled = 0
    for n, (place, piece) in enumerate(zip(places, pieces)):
        device = owner_of(place, me, devices)
        found = []
        if place == 0 and devices == GRID_DEVICES:
            found += [(l, l, None) for l in range(leaves)]
        for k in range(capacity):
            code = codes[0, 1, device * capacity + k].astype(jnp.int32)
            safe = jnp.maximum(code, 0)
            found.append((lax.rem(safe, leaves), lax.div(safe, leaves), code >= 0))
            code = codes[n + 1, 1, me * capacity + k].astype(jnp.int32)
            safe = jnp.maximum(code, 0)
            found.append((lax.div(safe, leaves), lax.rem(safe, leaves), code >= 0))
        if devices != GRID_DEVICES:
            found += [(l, l, device == me) for l in range(leaves)]
        for target, leaf, used in found:
            start = leaf * features
            if not isinstance(leaf, int):
                start = pl.multiple_of(start, features)
            sources[filled] = piece[pl.ds(start, features), :]
            rows[pl.ds(filled, 1), :] = piece[pl.ds(base + leaf, 1), :]
            targets[filled] = target
            vectors[filled] = device * leaves + leaf
            filled = filled + (1 if used is None else used.astype(jnp.int32))
    count[0] = filled
    for k in range(UNROLL):
        targets[filled + k] = leaves
        vectors[filled + k] = 0
        sources[filled + k] = pieces[0][:features, :]
        rows[pl.ds(filled + k, 1), :] = pieces[0][:1, :]

    def step(g, carry):
        found = []
        for k in range(UNROLL):
            n = g * UNROLL + k
            tile = tile_of(lefts[targets[n]], right_form(sources[n]))
            tiles[n] = tile
            found.append((n, tile * rows[pl.ds(n, 1), :]))
        for n, product in found:
            sums[targets[n]] += product
        return carry

    lax.fori_loop(0, (filled + UNROLL - 1) // UNROLL, step, 0)


def far_rows(sums, to_skel, to_top):
    leaves = to_skel.shape[0]
    mixed = jnp.sum(sums[leaves + 1], axis=1, keepdims=True)
    far, top = [], []
    for l in range(leaves):
        far.append(jnp.sum(to_skel[l] * jnp.sum(sums[l], axis=1, keepdims=True), axis=0, keepdims=True))
        top.append(jnp.sum(to_top[l] * mixed, axis=0, keepdims=True))
    return jnp.concatenate(far, axis=0), jnp.concatenate(top, axis=0)


def total_of(x):
    return jnp.sum(jnp.sum(x, axis=1, keepdims=True), axis=0, keepdims=True)


def in_lanes(*numbers):
    lane = lax.broadcasted_iota(jnp.int32, (1, 128), 1)
    row = jnp.zeros((1, 128), F32)
    for place, number in enumerate(numbers):
        row = jnp.where(lane == place, number, row)
    return row


def early_kernel(axis, devices, capacity, places, *refs):
    n = len(places)
    own_piece, pieces, lefts = refs[0], refs[1:n + 1], refs[n + 1]
    start = None
    if places[0] != 0:
        start, refs = refs[n + 2], refs[:n + 2] + refs[n + 3:]
    targets, vectors, count, tiles, tops, sums = refs[n + 2:n + 8]
    sums[...] = jnp.zeros_like(sums) if start is None else start[...]
    far_group(
        axis, devices, capacity, places, own_piece, pieces, lefts,
        (targets, vectors, count), tiles, tops, sums, refs[n + 8:],
    )


def first_kernel(reach, axis, devices, capacity, places, *refs):
    n = len(places)
    own_piece, pieces, lefts = refs[0], refs[1:n + 1], refs[n + 1]
    so_far, to_skel, to_top, values, near = refs[n + 2:n + 7]
    targets, vectors, count, tiles, tops, image, payload = refs[n + 7:n + 14]
    sums = refs[n + 14]
    sums[...] = so_far[...]
    far_group(
        axis, devices, capacity, places, own_piece, pieces, lefts,
        (targets, vectors, count), tiles, tops, sums, refs[n + 15:],
    )
    leaves, rank, size = to_skel.shape
    far, top = far_rows(sums, to_skel, to_top)
    start = values[...]
    result = start + 0.25 * near[...] + 0.125 * far + 0.25 * top
    image[...] = result
    coarse = jnp.zeros((rank, 128), F32)
    rows = []
    for l in range(leaves):
        row = result[l:l + 1, :]
        rows.append(as_row(folded(to_skel[l], row)))
        coarse = coarse + folded(to_top[l], row)
    rows.append(as_row(coarse))
    rows.append(in_lanes(total_of(start * start), total_of(start * result)))
    rows.append(jnp.zeros((16 - leaves - 2, 128), F32))
    for l in list(range(reach)) + list(range(leaves - reach, leaves)):
        rows += [result[l:l + 1, part:part + 128] for part in range(0, size, 128)]
    payload[...] = jnp.concatenate(rows, axis=0)


def beside_of(me, devices):
    return jnp.where(me == 0, devices - 1, me - 1), jnp.where(me == devices - 1, 0, me + 1)


def second_kernel(reach, axis, devices, groups, *refs):
    lists, refs = refs[:3 * len(groups)], refs[3 * len(groups):]
    tiles, refs = refs[:len(groups)], refs[len(groups):]
    tops, refs = refs[:len(groups)], refs[len(groups):]
    received, refs = refs[:1 if devices != GRID_DEVICES else 4], refs[1 if devices != GRID_DEVICES else 4:]
    to_skel, to_top, values, image, near, edges, residual, along, numbers, everyone, sums, across, beside = refs
    leaves, rank, size = to_skel.shape
    me = lax.axis_index(axis)
    if devices != GRID_DEVICES:
        everyone[...] = received[0][...]
    else:
        for other, blocks in enumerate(received):
            for turn in range(4):
                source = (((me >> 2) - turn + 4) & 3) * 4 + ((me & 3) ^ other)
                everyone[source] = blocks[turn]
    sums[...] = jnp.zeros_like(sums)
    for g, places in enumerate(groups):
        targets, vectors, count = lists[3 * g:3 * g + 3]

        def step(n, carry, g=g, targets=targets, vectors=vectors):
            products = []
            for k in range(UNROLL):
                vector = vectors[n * UNROLL + k]
                products.append(tiles[g][n * UNROLL + k] * everyone[lax.div(vector, leaves), pl.ds(lax.rem(vector, leaves), 1), :])
            for k in range(UNROLL):
                sums[targets[n * UNROLL + k]] += products[k]
            return carry

        lax.fori_loop(0, (count[0] + UNROLL - 1) // UNROLL, step, 0)
        for n, place in enumerate(places):
            device = owner_of(place, me, devices)
            sums[leaves + 1] += tops[g][n] * everyone[device, leaves:leaves + 1, :]
    far, top = far_rows(sums, to_skel, to_top)

    before, after = edges_of(leaves, reach)
    across[...] = jnp.zeros_like(across)
    beside[...] = jnp.zeros_like(beside)

    def edge_row(device, place):
        first = 16 + place * (size // 128)
        return jnp.concatenate([everyone[device, n:n + 1, :] for n in range(first, first + size // 128)], axis=1)

    behind, ahead = beside_of(me, devices)
    for n, (a, r) in enumerate(before):
        beside[a + 1 + r - reach] += backward(edges[n], down(edge_row(behind, reach + a)))
    for n, (a, r) in enumerate(after):
        row = edge_row(ahead, a + 1 + r - reach - leaves)
        across[a - leaves] += folded(edges[len(before) + n], row)
    extra = [jnp.sum(beside[r], axis=0, keepdims=True) for r in range(reach)]
    extra += [jnp.zeros((leaves - 2 * reach, size), F32)]
    extra += [as_row(across[r]) for r in range(reach)]
    start, first = values[...], image[...]
    near_all = near[...] + jnp.concatenate(extra, axis=0)
    second = first + 0.25 * near_all + 0.125 * far + 0.25 * top
    scalars = jnp.sum(everyone[:, leaves + 1, :], axis=0, keepdims=True)
    norm, product = scalars[:, 0:1], scalars[:, 1:2]
    alpha = norm / product
    left = start - alpha * first
    image_left = first - alpha * second
    residual[...] = left
    along[...] = image_left
    row = in_lanes(total_of(left * left), total_of(left * image_left), norm, alpha)
    numbers[...] = jnp.broadcast_to(row, numbers.shape)


def last_kernel(everyone, values, image, residual, along, solution_field, final):
    scalars = jnp.sum(everyone[:, 0, :], axis=0, keepdims=True)
    norm_next, product = scalars[:, 0:1], scalars[:, 1:2]
    norm, alpha = everyone[0, 0:1, 2:3], everyone[0, 0:1, 3:4]
    ratio = norm_next / norm
    step = norm_next / (product - ratio * norm_next / alpha)
    start, left = values[...], residual[...]
    solution_field[...] = alpha * start + step * (left + ratio * start)
    final[...] = left - step * (along[...] + ratio * image[...])


def shape(*dims, dtype=F32):
    return jax.ShapeDtypeStruct(dims, dtype)


SMEM = pl.BlockSpec(memory_space=pltpu.SMEM)
VMEM = pl.BlockSpec(memory_space=pltpu.VMEM)
ANY = pl.BlockSpec(memory_space=pl.ANY)
HBM = pl.BlockSpec(memory_space=pltpu.HBM)


def kernel_call(body, name, inputs, outputs, scratch=(), aliases={}, limit=VMEM_LIMIT, microseconds=1):
    out_specs, out_shapes = zip(*outputs)
    return pl.pallas_call(
        body,
        in_specs=list(inputs),
        out_specs=list(out_specs),
        out_shape=list(out_shapes),
        scratch_shapes=list(scratch),
        input_output_aliases=aliases,
        compiler_params=pltpu.CompilerParams(vmem_limit_bytes=limit),
        cost_estimate=pl.CostEstimate(
            flops=microseconds * 1_000_000_000, bytes_accessed=microseconds * 3_000_000, transcendentals=0
        ),
        name=name,
    )


def passed_along(block, axis, distance):
    size = lax.axis_size(axis)
    return lax.ppermute(block, axis, [((i - distance) % size, i) for i in range(size)])


def swapped(block, axis, bit):
    return lax.ppermute(block, axis, [(i, i ^ bit) for i in range(lax.axis_size(axis))])


def exchanged(blocks, axis):
    return lax.all_to_all(blocks, axis, split_axis=0, concat_axis=0, tiled=True)


def gathered_blocks(block, axis):
    devices = lax.axis_size(axis)
    if devices != GRID_DEVICES:
        return [exchanged(jnp.broadcast_to(block[None], (devices,) + block.shape), axis)]
    turned = jnp.stack([block] + [passed_along(block, axis, 4 * turn) for turn in (1, 2, 3)])
    return [turned] + [swapped(turned, axis, other) for other in (1, 2, 3)]


def all_pieces(piece, again, axis):
    devices = lax.axis_size(axis)
    if devices != GRID_DEVICES:
        together = lax.all_gather(piece[None], axis, axis=0, tiled=True)
        return [together[n] for n in range(devices)]
    turned = {0: piece}
    for turn in (1, 3, 2):
        turned[turn] = passed_along(again if turn == 2 else piece, axis, 4 * turn)
    pieces = []
    for turn, across in ORDER:
        mine = swapped(turned[turn], axis, 2) if across else turned[turn]
        pieces += [mine, swapped(mine, axis, 1)]
    return pieces


def on_device(points, right_side, near_mask, far_dest, far_leaf, skeleton, top_index):
    leaves, features, size = points.shape
    reach = near_mask.shape[1]
    fan_out = far_dest.shape[1]
    rank = skeleton.shape[1]
    devices = lax.axis_size("leaf")
    capacity = max(2, (2 * leaves * fan_out + devices - 1) // devices)
    depth = 3 * features + 16
    piece_rows = (leaves + 1) * features + 16
    halo_rows = features + 8
    integers = jnp.int32
    payload_rows = 16 + 2 * reach * size // rank

    piece, again, to_skel, to_top, lefts, first, last = kernel_call(
        functools.partial(prepare_kernel, devices, capacity),
        "prepare",
        [HBM] * 7,
        [
            (VMEM, shape(piece_rows, rank)),
            (VMEM, shape(piece_rows, rank)),
            (VMEM, shape(leaves, rank, size)),
            (VMEM, shape(leaves, rank, size)),
            (VMEM, shape(leaves + 1, depth, rank, dtype=BF16)),
            (VMEM, shape(reach, halo_rows, size)),
            (VMEM, shape(reach, halo_rows, size)),
        ],
        [
            pltpu.VMEM(points.shape, F32),
            pltpu.VMEM(right_side.shape, F32),
            pltpu.VMEM(near_mask.T.shape, integers),
            pltpu.VMEM(skeleton.shape, integers),
            pltpu.VMEM(top_index.shape, integers),
            pltpu.VMEM(far_dest.T.shape, integers),
            pltpu.VMEM(far_leaf.T.shape, integers),
            pltpu.VMEM((leaves, depth, size), BF16),
            pltpu.SemaphoreType.DMA((7,)),
        ],
        limit=60 * 1024 * 1024,
        microseconds=2,
    )(points, right_side, near_mask.T, skeleton, top_index, far_dest.T, far_leaf.T)

    following = passed_along(first, "leaf", -1)
    preceding = passed_along(last, "leaf", 1)
    def near_apply(halo, values, *others):
        before, after = edges_of(leaves, reach)
        outputs = [(VMEM, shape(leaves, size))]
        if halo:
            outputs.append((VMEM, shape(len(before) + len(after), size, size)))
            outputs.append((ANY, shape(piece_rows, rank)))
        return kernel_call(
            functools.partial(near_kernel, halo),
            "near_first" if halo else "near_second",
            [VMEM, VMEM, SMEM] + [VMEM, VMEM, ANY][:len(others)],
            outputs,
            [
                pltpu.VMEM((leaves + reach, depth, size), BF16),
                pltpu.VMEM((leaves + 2 * reach, depth, size), BF16),
                pltpu.VMEM((leaves + reach, size, 128), F32),
                pltpu.VMEM((leaves, size, 128), F32),
                pltpu.VMEM((leaves, 8, size), F32),
            ],
            {5: 2} if halo else {},
            microseconds=5,
        )(points, values, near_mask.T, *others)

    near, edges, again = near_apply(True, right_side, following, preceding, again)
    pieces = all_pieces(piece, again, "leaf")
    cuts = (0, devices // 2, devices * 7 // 8, devices)
    groups = [tuple(range(start, end)) for start, end in zip(cuts, cuts[1:])]
    sums = shape(leaves + 2, rank, rank)

    def group_call(body, name, places, inputs, outputs, scratch):
        most = -(-(2 * capacity * len(places) + leaves + UNROLL) // UNROLL) * UNROLL
        return kernel_call(
            functools.partial(body, "leaf", devices, capacity, places),
            name,
            [ANY] + [VMEM] * (len(places) + 1 + len(inputs)),
            [
                (SMEM, shape(most, dtype=integers)),
                (SMEM, shape(most, dtype=integers)),
                (SMEM, shape(1, dtype=integers)),
                (VMEM, shape(most, rank, rank)),
                (VMEM, shape(len(places), rank, rank)),
            ] + outputs,
            scratch + [
                pltpu.VMEM((most, features, rank), F32),
                pltpu.VMEM((most, rank), F32),
                pltpu.SMEM((len(places) + 1, 8, 128), F32),
                pltpu.SemaphoreType.DMA((len(places) + 1,)),
            ],
            microseconds=1 + len(places),
        )(piece, *[pieces[place] for place in places], lefts, *inputs)

    early = group_call(early_kernel, "far_early", groups[0], [], [(VMEM, sums)], [])
    middle = group_call(early_kernel, "far_middle", groups[1], [early[5]], [(VMEM, sums)], [])
    late = group_call(
        functools.partial(first_kernel, reach),
        "far_late",
        groups[2],
        [middle[5], to_skel, to_top, right_side, near],
        [(VMEM, shape(leaves, size)), (VMEM, shape(payload_rows, rank))],
        [pltpu.VMEM(sums.shape, F32)],
    )
    image, payload = late[5:]

    everyone = gathered_blocks(payload, "leaf")
    near_second = near_apply(False, image)[0]
    residual, along, numbers = kernel_call(
        functools.partial(second_kernel, reach, "leaf", devices, groups),
        "far_second",
        [SMEM] * 9 + [VMEM] * (12 + len(everyone)),
        [
            (VMEM, shape(leaves, size)),
            (VMEM, shape(leaves, size)),
            (VMEM, shape(devices, 1, 128)),
        ],
        [
            pltpu.VMEM((devices, payload_rows, rank), F32),
            pltpu.VMEM(sums.shape, F32),
            pltpu.VMEM((reach, size, 128), F32),
            pltpu.VMEM((reach, 8, size), F32),
        ],
    )(
        *early[:3], *middle[:3], *late[:3], early[3], middle[3], late[3], early[4], middle[4], late[4],
        *everyone, to_skel, to_top, right_side, image, near_second, edges,
    )

    solution_field, final = kernel_call(
        last_kernel,
        "finish",
        [VMEM] * 5,
        [(VMEM, shape(leaves, size)), (VMEM, shape(leaves, size))],
    )(exchanged(numbers, "leaf"), right_side, image, residual, along)
    return solution_field, final


def solution(mesh):
    rows = P(("groups", "leaf"), None)
    in_specs = (P(("groups", "leaf"), None, None),) + (rows,) * 6
    return jax.shard_map(
        on_device, mesh=mesh, in_specs=in_specs, out_specs=(rows, rows), check_vma=False
    )
```

```python
import functools
import math

import jax
import jax.numpy as jnp
from jax import lax
from jax.experimental import pallas as pl
from jax.experimental.pallas import tpu as pltpu
from jax.sharding import PartitionSpec as P

F32 = jnp.float32
BF16 = jnp.bfloat16
VMEM_LIMIT = 20 * 1024 * 1024
UNROLL = 4
GRID_DEVICES = 16
ORDER = ((0, 0), (0, 1), (1, 0), (1, 1), (2, 0), (2, 1), (3, 0), (3, 1))
CUTS = (0, 6, 10, 14, 16)


def contract_first(left, right):
    return lax.dot_general(left, right, (((0,), (0,)), ((), ())), preferred_element_type=F32)


def halves(x):
    high = x.astype(BF16)
    return high, (x - high.astype(F32)).astype(BF16)


def thirds(x):
    high = x.astype(BF16)
    rest = x - high.astype(F32)
    middle = rest.astype(BF16)
    return high, middle, (rest - middle.astype(F32)).astype(BF16)


def norm_rows(x, factor, first):
    norm = jnp.sum(x * x, axis=0, keepdims=True) * factor
    high, middle, low = [piece.astype(F32) for piece in thirds(norm)]
    row = lax.broadcasted_iota(jnp.int32, (16, x.shape[1]), 0)
    rows = jnp.where(row < 6, 1.0, 0.0)
    for place, piece in ((first, high), (first + 1, middle), (first + 2, low)):
        rows = jnp.where(row == place, piece, rows)
    return rows.astype(BF16)


def unit(features):
    return 2.0 / features * math.log2(math.e)


def right_form(x):
    high, low = halves(x)
    return jnp.concatenate([high, high, low, norm_rows(x, -unit(x.shape[0]), 0)], axis=0)


def left_form(x):
    high, low = halves(x * (2.0 * unit(x.shape[0])))
    return jnp.concatenate([high, low, high, norm_rows(x, -unit(x.shape[0]), 3)], axis=0)


def tile_of(left, right):
    return jnp.exp2(contract_first(left, right))


def folded(tile, row):
    total = tile[:, :128] * row[:, :128]
    for start in range(128, tile.shape[1], 128):
        total = total + tile[:, start:start + 128] * row[:, start:start + 128]
    return total


def as_row(matrix):
    return jnp.sum(matrix.T, axis=0, keepdims=True)


def down(row):
    return jnp.broadcast_to(row, (128, row.shape[1])).T


def wide(column_matrix, columns):
    return jnp.concatenate([column_matrix] * (columns // 128), axis=1)


def owner_of(place, me, devices):
    if devices != GRID_DEVICES:
        return place
    turn, across = ORDER[place // 2]
    return (((me >> 2) - turn + 4) & 3) * 4 + ((me & 3) ^ (2 * across + place % 2))


def prepare_kernel(devices, capacity, *refs):
    (points_in, values_in, mask_in, skeleton_in, top_in, dest_in, leaf_in) = refs[:7]
    piece, to_skel, to_top, lefts, first, last = refs[7:13]
    points, values, mask, skeleton, top, dest, leaf, rights, sems = refs[13:]
    copies = []
    for n, (source, target) in enumerate(zip(refs[:7], (points, values, mask, skeleton, top, dest, leaf))):
        copies.append(pltpu.make_async_copy(source, target, sems.at[n]))
        copies[-1].start()
    for copy in copies:
        copy.wait()
    leaves, features, size = points.shape
    reach = first.shape[0]
    rank = skeleton.shape[1]
    fan_out = dest.shape[0]
    pad = first.shape[1] - features - 1 - reach
    top_total = jnp.zeros((3 * features, rank), F32)
    spot = lax.broadcasted_iota(jnp.int32, (size, rank), 0)
    for l in range(leaves):
        x = points[l]
        chosen = jnp.concatenate(
            [spot == skeleton[l:l + 1, :], spot == top[...] - l * size], axis=1
        )
        picked = jnp.dot(
            jnp.concatenate(thirds(x), axis=0),
            jnp.where(chosen, 1.0, 0.0).astype(BF16),
            preferred_element_type=F32,
        )
        skel = picked[:, :rank]
        skel = skel[:features] + skel[features:2 * features] + skel[2 * features:]
        piece[l * features:(l + 1) * features, :] = skel
        lefts[l] = left_form(skel)
        rights[l] = right_form(x)
        top_total = top_total + picked[:, rank:]
    chosen_top = top_total[:features] + top_total[features:2 * features] + top_total[2 * features:]
    piece[leaves * features:(leaves + 1) * features, :] = chosen_top
    lefts[leaves] = left_form(chosen_top)
    coarse = jnp.zeros((rank, 128), F32)
    base = (leaves + 1) * features
    for l in range(leaves):
        both = tile_of(jnp.concatenate([lefts[l], lefts[leaves]], axis=1), rights[l])
        to_skel[l] = both[:rank]
        to_top[l] = both[rank:]
        row = values[l:l + 1, :]
        piece[base + l:base + l + 1, :] = as_row(folded(both[:rank], row))
        coarse = coarse + folded(both[rank:], row)
    lane = lax.broadcasted_iota(jnp.int32, (1, 128), 1)
    codes = jnp.full((1, 128), -1.0, F32)
    seen = jnp.zeros((1, 128), jnp.int32)
    for l in range(leaves):
        for f in range(fan_out):
            here = lax.div(lane, jnp.int32(capacity)) == dest[f:f + 1, l:l + 1]
            code = (leaf[f:f + 1, l:l + 1] * leaves + l).astype(F32)
            codes = jnp.where(here & (lax.rem(lane, jnp.int32(capacity)) == seen), code, codes)
            seen = seen + here.astype(jnp.int32)
    piece[base + leaves:base + leaves + 8, :] = jnp.concatenate(
        [as_row(coarse), codes, jnp.zeros((6, 128), F32)], axis=0
    )
    for r in range(reach):
        first[r, :features, :] = points[r]
        last[r, :features, :] = points[leaves - reach + r]
        first[r, features:, :] = jnp.broadcast_to(values[r:r + 1, :], (first.shape[1] - features, size))
        own = leaves - reach + r
        rows = [values[own:own + 1, :]]
        rows += [jnp.broadcast_to(mask[s:s + 1, own:own + 1].astype(F32), (1, size)) for s in range(reach)]
        last[r, features:, :] = jnp.concatenate(rows + [jnp.zeros((pad, size), F32)], axis=0)


def edges_of(leaves, reach):
    pairs = [(a, r) for a in range(leaves + reach) for r in range(reach)]
    before = [(a, r) for a, r in pairs if a < reach <= a + 1 + r]
    after = [(a, r) for a, r in pairs if a >= reach and a + 1 + r >= leaves + reach]
    return before, after


def backward(tile, column):
    size = tile.shape[1]
    return jnp.sum((tile * wide(column, size)).reshape(-1, 8, size), axis=0)


def near_kernel(halo, points, values, mask, *refs):
    leaves, features, size = points.shape
    if halo:
        following, preceding, out, edges, lefts, rights, downs, across, along = refs
    else:
        out, lefts, rights, downs, across, along = refs
    reach = mask.shape[0]
    before, after = edges_of(leaves, reach)

    def block(e):
        if e < reach:
            return preceding[e, :features, :]
        if e < reach + leaves:
            return points[e - reach]
        return following[e - reach - leaves, :features, :]

    def row_of(e):
        if e < reach:
            return preceding[e, features:features + 1, :]
        if e < reach + leaves:
            return values[e - reach:e - reach + 1, :]
        return following[e - reach - leaves, features:features + 1, :]

    for e in range(leaves + 2 * reach):
        own = reach <= e < leaves + reach
        if own or halo:
            x = block(e)
            if e < leaves + reach:
                lefts[e] = left_form(x)
                downs[e] = down(row_of(e))
            if e >= reach:
                rights[e] = right_form(x)
    for l in range(leaves):
        e = l + reach
        along[l] = backward(tile_of(lefts[e], rights[e]), downs[e])
        across[l] = jnp.zeros((size, 128), F32)
    for a in range(leaves + reach):
        for r in range(reach):
            b = a + 1 + r
            if a >= reach and b < leaves + reach:
                @pl.when(mask[r, a - reach] != 0)
                def _(a=a, b=b):
                    tile = tile_of(lefts[a], rights[b])
                    across[a - reach] += folded(tile, row_of(b))
                    along[b - reach] += backward(tile, downs[a])
    if halo:
        for n, (a, r) in enumerate(before):
            b = a + 1 + r
            tile = tile_of(lefts[a], rights[b]) * preceding[a, features + 1 + r:features + 2 + r, :]
            edges[n] = tile
            along[b - reach] += backward(tile, downs[a])
        for n, (a, r) in enumerate(after):
            b = a + 1 + r
            place = len(before) + n

            @pl.when(mask[r, a - reach] == 0)
            def _(place=place):
                edges[place] = jnp.zeros((size, size), F32)

            @pl.when(mask[r, a - reach] != 0)
            def _(a=a, b=b, place=place):
                tile = tile_of(lefts[a], rights[b])
                edges[place] = tile
                across[a - reach] += folded(tile, row_of(b))

    for l in range(leaves):
        out[l:l + 1, :] = as_row(across[l]) + jnp.sum(along[l], axis=0, keepdims=True)


def far_group(axis, devices, capacity, places, own_piece, pieces, lefts, lists, tiles, tops, sums, scratch):
    targets, vectors, count = lists
    sources, rows, codes, sems = scratch
    leaves = lefts.shape[0] - 1
    features = (pieces[0].shape[0] - 16) // (leaves + 1)
    base = (leaves + 1) * features
    me = lax.axis_index(axis)
    copies = [
        pltpu.make_async_copy(ref.at[base + 8:base + 16, :], codes.at[n], sems.at[n])
        for n, ref in enumerate([own_piece] + list(pieces))
    ]
    for copy in copies:
        copy.start()
    for n, piece in enumerate(pieces):
        tile = tile_of(lefts[leaves], right_form(piece[leaves * features:(leaves + 1) * features, :]))
        tops[n] = tile
        sums[leaves + 1] += tile * piece[base + leaves:base + leaves + 1, :]
    for copy in copies:
        copy.wait()
    filled = 0
    for n, (place, piece) in enumerate(zip(places, pieces)):
        device = owner_of(place, me, devices)
        found = []
        if place == 0 and devices == GRID_DEVICES:
            found += [(l, l, None) for l in range(leaves)]
        for k in range(capacity):
            code = codes[0, 1, device * capacity + k].astype(jnp.int32)
            safe = jnp.maximum(code, 0)
            found.append((lax.rem(safe, leaves), lax.div(safe, leaves), code >= 0))
            code = codes[n + 1, 1, me * capacity + k].astype(jnp.int32)
            safe = jnp.maximum(code, 0)
            found.append((lax.div(safe, leaves), lax.rem(safe, leaves), code >= 0))
        if devices != GRID_DEVICES:
            found += [(l, l, device == me) for l in range(leaves)]
        for target, leaf, used in found:
            start = leaf * features
            if not isinstance(leaf, int):
                start = pl.multiple_of(start, features)
            sources[filled] = piece[pl.ds(start, features), :]
            rows[pl.ds(filled, 1), :] = piece[pl.ds(base + leaf, 1), :]
            targets[filled] = target
            vectors[filled] = device * leaves + leaf
            filled = filled + (1 if used is None else used.astype(jnp.int32))
    count[0] = filled
    for k in range(UNROLL):
        targets[filled + k] = leaves
        vectors[filled + k] = 0
        sources[filled + k] = pieces[0][:features, :]
        rows[pl.ds(filled + k, 1), :] = pieces[0][:1, :]

    def step(g, carry):
        found = []
        for k in range(UNROLL):
            n = g * UNROLL + k
            tile = tile_of(lefts[targets[n]], right_form(sources[n]))
            tiles[n] = tile
            found.append((n, tile * rows[pl.ds(n, 1), :]))
        for n, product in found:
            sums[targets[n]] += product
        return carry

    lax.fori_loop(0, (filled + UNROLL - 1) // UNROLL, step, 0)


def far_rows(sums, to_skel, to_top):
    leaves = to_skel.shape[0]
    mixed = jnp.sum(sums[leaves + 1], axis=1, keepdims=True)
    far, top = [], []
    for l in range(leaves):
        far.append(jnp.sum(to_skel[l] * jnp.sum(sums[l], axis=1, keepdims=True), axis=0, keepdims=True))
        top.append(jnp.sum(to_top[l] * mixed, axis=0, keepdims=True))
    return jnp.concatenate(far, axis=0), jnp.concatenate(top, axis=0)


def total_of(x):
    return jnp.sum(jnp.sum(x, axis=1, keepdims=True), axis=0, keepdims=True)


def in_lanes(*numbers):
    lane = lax.broadcasted_iota(jnp.int32, (1, 128), 1)
    row = jnp.zeros((1, 128), F32)
    for place, number in enumerate(numbers):
        row = jnp.where(lane == place, number, row)
    return row


def early_kernel(axis, devices, capacity, places, *refs):
    n = len(places)
    own_piece, pieces, lefts = refs[0], refs[1:n + 1], refs[n + 1]
    start = None
    if places[0] != 0:
        start, refs = refs[n + 2], refs[:n + 2] + refs[n + 3:]
    targets, vectors, count, tiles, tops, sums = refs[n + 2:n + 8]
    sums[...] = jnp.zeros_like(sums) if start is None else start[...]
    far_group(
        axis, devices, capacity, places, own_piece, pieces, lefts,
        (targets, vectors, count), tiles, tops, sums, refs[n + 8:],
    )


def first_kernel(reach, axis, devices, capacity, places, *refs):
    n = len(places)
    own_piece, pieces, lefts = refs[0], refs[1:n + 1], refs[n + 1]
    so_far, to_skel, to_top, values, near = refs[n + 2:n + 7]
    targets, vectors, count, tiles, tops, image, payload = refs[n + 7:n + 14]
    sums = refs[n + 14]
    sums[...] = so_far[...]
    far_group(
        axis, devices, capacity, places, own_piece, pieces, lefts,
        (targets, vectors, count), tiles, tops, sums, refs[n + 15:],
    )
    leaves, rank, size = to_skel.shape
    far, top = far_rows(sums, to_skel, to_top)
    start = values[...]
    result = start + 0.25 * near[...] + 0.125 * far + 0.25 * top
    image[...] = result
    coarse = jnp.zeros((rank, 128), F32)
    rows = []
    for l in range(leaves):
        row = result[l:l + 1, :]
        rows.append(as_row(folded(to_skel[l], row)))
        coarse = coarse + folded(to_top[l], row)
    rows.append(as_row(coarse))
    rows.append(in_lanes(total_of(start * start), total_of(start * result)))
    rows.append(jnp.zeros((16 - leaves - 2, 128), F32))
    for l in list(range(reach)) + list(range(leaves - reach, leaves)):
        rows += [result[l:l + 1, part:part + 128] for part in range(0, size, 128)]
    payload[...] = jnp.concatenate(rows, axis=0)


def beside_of(me, devices):
    return jnp.where(me == 0, devices - 1, me - 1), jnp.where(me == devices - 1, 0, me + 1)


def second_kernel(reach, axis, devices, groups, *refs):
    lists, refs = refs[:3 * len(groups)], refs[3 * len(groups):]
    tiles, refs = refs[:len(groups)], refs[len(groups):]
    tops, refs = refs[:len(groups)], refs[len(groups):]
    received, refs = refs[:1 if devices != GRID_DEVICES else 4], refs[1 if devices != GRID_DEVICES else 4:]
    to_skel, to_top, values, image, near, edges, residual, along, numbers, everyone, sums, across, beside = refs
    leaves, rank, size = to_skel.shape
    me = lax.axis_index(axis)
    if devices != GRID_DEVICES:
        everyone[...] = received[0][...]
    else:
        for other, blocks in enumerate(received):
            for turn in range(4):
                source = (((me >> 2) - turn + 4) & 3) * 4 + ((me & 3) ^ other)
                everyone[source] = blocks[turn]
    sums[...] = jnp.zeros_like(sums)
    for g, places in enumerate(groups):
        targets, vectors, count = lists[3 * g:3 * g + 3]

        def step(n, carry, g=g, targets=targets, vectors=vectors):
            products = []
            for k in range(UNROLL):
                vector = vectors[n * UNROLL + k]
                products.append(tiles[g][n * UNROLL + k] * everyone[lax.div(vector, leaves), pl.ds(lax.rem(vector, leaves), 1), :])
            for k in range(UNROLL):
                sums[targets[n * UNROLL + k]] += products[k]
            return carry

        lax.fori_loop(0, (count[0] + UNROLL - 1) // UNROLL, step, 0)
        for n, place in enumerate(places):
            device = owner_of(place, me, devices)
            sums[leaves + 1] += tops[g][n] * everyone[device, leaves:leaves + 1, :]
    far, top = far_rows(sums, to_skel, to_top)

    before, after = edges_of(leaves, reach)
    across[...] = jnp.zeros_like(across)
    beside[...] = jnp.zeros_like(beside)

    def edge_row(device, place):
        first = 16 + place * (size // 128)
        return jnp.concatenate([everyone[device, n:n + 1, :] for n in range(first, first + size // 128)], axis=1)

    behind, ahead = beside_of(me, devices)
    for n, (a, r) in enumerate(before):
        beside[a + 1 + r - reach] += backward(edges[n], down(edge_row(behind, reach + a)))
    for n, (a, r) in enumerate(after):
        row = edge_row(ahead, a + 1 + r - reach - leaves)
        across[a - leaves] += folded(edges[len(before) + n], row)
    extra = [jnp.sum(beside[r], axis=0, keepdims=True) for r in range(reach)]
    extra += [jnp.zeros((leaves - 2 * reach, size), F32)]
    extra += [as_row(across[r]) for r in range(reach)]
    start, first = values[...], image[...]
    near_all = near[...] + jnp.concatenate(extra, axis=0)
    second = first + 0.25 * near_all + 0.125 * far + 0.25 * top
    scalars = jnp.sum(everyone[:, leaves + 1, :], axis=0, keepdims=True)
    norm, product = scalars[:, 0:1], scalars[:, 1:2]
    alpha = norm / product
    left = start - alpha * first
    image_left = first - alpha * second
    residual[...] = left
    along[...] = image_left
    row = in_lanes(total_of(left * left), total_of(left * image_left), norm, alpha)
    numbers[...] = jnp.broadcast_to(row, numbers.shape)


def last_kernel(everyone, values, image, residual, along, solution_field, final):
    scalars = jnp.sum(everyone[:, 0, :], axis=0, keepdims=True)
    norm_next, product = scalars[:, 0:1], scalars[:, 1:2]
    norm, alpha = everyone[0, 0:1, 2:3], everyone[0, 0:1, 3:4]
    ratio = norm_next / norm
    step = norm_next / (product - ratio * norm_next / alpha)
    start, left = values[...], residual[...]
    solution_field[...] = alpha * start + step * (left + ratio * start)
    final[...] = left - step * (along[...] + ratio * image[...])


def shape(*dims, dtype=F32):
    return jax.ShapeDtypeStruct(dims, dtype)


SMEM = pl.BlockSpec(memory_space=pltpu.SMEM)
VMEM = pl.BlockSpec(memory_space=pltpu.VMEM)
ANY = pl.BlockSpec(memory_space=pl.ANY)
HBM = pl.BlockSpec(memory_space=pltpu.HBM)


def kernel_call(body, name, inputs, outputs, scratch=(), aliases={}, limit=VMEM_LIMIT, microseconds=1):
    out_specs, out_shapes = zip(*outputs)
    return pl.pallas_call(
        body,
        in_specs=list(inputs),
        out_specs=list(out_specs),
        out_shape=list(out_shapes),
        scratch_shapes=list(scratch),
        input_output_aliases=aliases,
        compiler_params=pltpu.CompilerParams(vmem_limit_bytes=limit),
        cost_estimate=pl.CostEstimate(
            flops=int(microseconds * 1_000_000_000), bytes_accessed=int(microseconds * 3_000_000), transcendentals=0
        ),
        name=name,
    )


def passed_along(block, axis, distance):
    size = lax.axis_size(axis)
    return lax.ppermute(block, axis, [((i - distance) % size, i) for i in range(size)])


def swapped(block, axis, bit):
    return lax.ppermute(block, axis, [(i, i ^ bit) for i in range(lax.axis_size(axis))])


def exchanged(blocks, axis):
    return lax.all_to_all(blocks, axis, split_axis=0, concat_axis=0, tiled=True)


def gathered_blocks(block, axis):
    devices = lax.axis_size(axis)
    if devices != GRID_DEVICES:
        return [exchanged(jnp.broadcast_to(block[None], (devices,) + block.shape), axis)]
    turned = jnp.stack([block] + [passed_along(block, axis, 4 * turn) for turn in (1, 2, 3)])
    return [turned] + [swapped(turned, axis, other) for other in (1, 2, 3)]


def on_device(points, right_side, near_mask, far_dest, far_leaf, skeleton, top_index):
    leaves, features, size = points.shape
    reach = near_mask.shape[1]
    fan_out = far_dest.shape[1]
    rank = skeleton.shape[1]
    devices = lax.axis_size("leaf")
    capacity = max(2, (2 * leaves * fan_out + devices - 1) // devices)
    depth = 3 * features + 16
    piece_rows = (leaves + 1) * features + 16
    halo_rows = features + 8
    integers = jnp.int32
    payload_rows = 16 + 2 * reach * size // rank

    piece, to_skel, to_top, lefts, first, last = kernel_call(
        functools.partial(prepare_kernel, devices, capacity),
        "prepare",
        [HBM] * 7,
        [
            (VMEM, shape(piece_rows, rank)),
            (VMEM, shape(leaves, rank, size)),
            (VMEM, shape(leaves, rank, size)),
            (VMEM, shape(leaves + 1, depth, rank, dtype=BF16)),
            (VMEM, shape(reach, halo_rows, size)),
            (VMEM, shape(reach, halo_rows, size)),
        ],
        [
            pltpu.VMEM(points.shape, F32),
            pltpu.VMEM(right_side.shape, F32),
            pltpu.VMEM(near_mask.T.shape, integers),
            pltpu.VMEM(skeleton.shape, integers),
            pltpu.VMEM(top_index.shape, integers),
            pltpu.VMEM(far_dest.T.shape, integers),
            pltpu.VMEM(far_leaf.T.shape, integers),
            pltpu.VMEM((leaves, depth, size), BF16),
            pltpu.SemaphoreType.DMA((7,)),
        ],
        limit=60 * 1024 * 1024,
        microseconds=2,
    )(points, right_side, near_mask.T, skeleton, top_index, far_dest.T, far_leaf.T)

    following = passed_along(first, "leaf", -1)
    preceding = passed_along(last, "leaf", 1)
    def near_apply(halo, values, *others):
        before, after = edges_of(leaves, reach)
        outputs = [(VMEM, shape(leaves, size))]
        if halo:
            outputs.append((VMEM, shape(len(before) + len(after), size, size)))
        return kernel_call(
            functools.partial(near_kernel, halo),
            "near_first" if halo else "near_second",
            [VMEM, VMEM, SMEM] + [VMEM] * len(others),
            outputs,
            [
                pltpu.VMEM((leaves + reach, depth, size), BF16),
                pltpu.VMEM((leaves + 2 * reach, depth, size), BF16),
                pltpu.VMEM((leaves + reach, size, 128), F32),
                pltpu.VMEM((leaves, size, 128), F32),
                pltpu.VMEM((leaves, 8, size), F32),
            ],
            microseconds=3 if halo else 4,
        )(points, values, near_mask.T, *others)

    near, edges = near_apply(True, right_side, following, preceding)
    cuts = [devices * cut // GRID_DEVICES for cut in CUTS]
    groups = [tuple(range(start, end)) for start, end in zip(cuts, cuts[1:])]
    if devices == GRID_DEVICES:
        pieces = {}
    else:
        together = lax.all_gather(piece[None], "leaf", axis=0, tiled=True)
        pieces = {place: together[place] for place in range(devices)}
    sums = shape(leaves + 2, rank, rank)

    def group_call(body, name, places, inputs, outputs, scratch):
        most = -(-(2 * capacity * len(places) + leaves + UNROLL) // UNROLL) * UNROLL
        return kernel_call(
            functools.partial(body, "leaf", devices, capacity, places),
            name,
            [ANY] + [VMEM] * (len(places) + 1 + len(inputs)),
            [
                (SMEM, shape(most, dtype=integers)),
                (SMEM, shape(most, dtype=integers)),
                (SMEM, shape(1, dtype=integers)),
                (VMEM, shape(most, rank, rank)),
                (VMEM, shape(len(places), rank, rank)),
            ] + outputs,
            scratch + [
                pltpu.VMEM((most, features, rank), F32),
                pltpu.VMEM((most, rank), F32),
                pltpu.SMEM((len(places) + 1, 8, 128), F32),
                pltpu.SemaphoreType.DMA((len(places) + 1,)),
            ],
            microseconds={0: 7, 6: 5, 10: 3}.get(places[0], 3),
        )(piece, *[pieces[place] for place in places], lefts, *inputs)

    def hold(value, *others):
        return lax.optimization_barrier((value, *others))[0]

    def put(slot, value):
        pieces[2 * slot] = value
        pieces[2 * slot + 1] = swapped(value, "leaf", 1)

    passes = []

    def tiles_of_group():
        number = len(passes)
        start = [passes[-1][5]] if passes else []
        passes.append(
            group_call(early_kernel, "far_tiles_%d" % number, groups[number], start, [(VMEM, sums)], [])
        )
        return passes[-1][5]

    if devices == GRID_DEVICES:
        put(0, piece)
        put(1, swapped(piece, "leaf", 2))
        turned = passed_along(piece, "leaf", 4)
        put(2, turned)
        across = swapped(turned, "leaf", 2)
        turned = hold(passed_along(turned, "leaf", 4), tiles_of_group())
        put(3, across)
        put(4, turned)
        across = swapped(turned, "leaf", 2)
        turned = hold(passed_along(turned, "leaf", 4), tiles_of_group())
        put(5, across)
        put(6, turned)
        put(7, hold(swapped(turned, "leaf", 2), tiles_of_group(), near))
    else:
        for _ in groups[:-1]:
            tiles_of_group()
    late = group_call(
        functools.partial(first_kernel, reach),
        "far_last",
        groups[3],
        [passes[-1][5], to_skel, to_top, right_side, near],
        [(VMEM, shape(leaves, size)), (VMEM, shape(payload_rows, rank))],
        [pltpu.VMEM(sums.shape, F32)],
    )
    passes.append(late)
    image, payload = late[5:]

    everyone = gathered_blocks(payload, "leaf")
    near_second = near_apply(False, image)[0]
    residual, along, numbers = kernel_call(
        functools.partial(second_kernel, reach, "leaf", devices, groups),
        "far_second",
        [SMEM] * (3 * len(groups)) + [VMEM] * (2 * len(groups) + 6 + len(everyone)),
        [
            (VMEM, shape(leaves, size)),
            (VMEM, shape(leaves, size)),
            (VMEM, shape(devices, 1, 128)),
        ],
        [
            pltpu.VMEM((devices, payload_rows, rank), F32),
            pltpu.VMEM(sums.shape, F32),
            pltpu.VMEM((reach, size, 128), F32),
            pltpu.VMEM((reach, 8, size), F32),
        ],
    )(
        *[table for done in passes for table in done[:3]],
        *[done[3] for done in passes],
        *[done[4] for done in passes],
        *everyone, to_skel, to_top, right_side, image, near_second, edges,
    )

    solution_field, final = kernel_call(
        last_kernel,
        "finish",
        [VMEM] * 5,
        [(VMEM, shape(leaves, size)), (VMEM, shape(leaves, size))],
    )(exchanged(numbers, "leaf"), right_side, image, residual, along)
    return solution_field, final


def solution(mesh):
    rows = P(("groups", "leaf"), None)
    in_specs = (P(("groups", "leaf"), None, None),) + (rows,) * 6
    return jax.shard_map(
        on_device, mesh=mesh, in_specs=in_specs, out_specs=(rows, rows), check_vma=False
    )
```

```python
import functools
import math

import jax
import jax.numpy as jnp
from jax import lax
from jax.experimental import pallas as pl
from jax.experimental.pallas import tpu as pltpu
from jax.sharding import PartitionSpec as P

F32 = jnp.float32
BF16 = jnp.bfloat16
VMEM_LIMIT = 20 * 1024 * 1024
UNROLL = 4
GRID_DEVICES = 16
ORDER = ((0, 0), (0, 1), (1, 0), (1, 1), (2, 0), (2, 1), (3, 0), (3, 1))
CUTS = (0, 6, 10, 14, 16)


def contract_first(left, right):
    return lax.dot_general(left, right, (((0,), (0,)), ((), ())), preferred_element_type=F32)


def halves(x):
    high = x.astype(BF16)
    return high, (x - high.astype(F32)).astype(BF16)


def thirds(x):
    high = x.astype(BF16)
    rest = x - high.astype(F32)
    middle = rest.astype(BF16)
    return high, middle, (rest - middle.astype(F32)).astype(BF16)


def norm_rows(x, factor, first):
    norm = jnp.sum(x * x, axis=0, keepdims=True) * factor
    high, middle, low = [piece.astype(F32) for piece in thirds(norm)]
    row = lax.broadcasted_iota(jnp.int32, (16, x.shape[1]), 0)
    rows = jnp.where(row < 6, 1.0, 0.0)
    for place, piece in ((first, high), (first + 1, middle), (first + 2, low)):
        rows = jnp.where(row == place, piece, rows)
    return rows.astype(BF16)


def unit(features):
    return 2.0 / features * math.log2(math.e)


def right_form(x):
    high, low = halves(x)
    return jnp.concatenate([high, high, low, norm_rows(x, -unit(x.shape[0]), 0)], axis=0)


def left_form(x):
    high, low = halves(x * (2.0 * unit(x.shape[0])))
    return jnp.concatenate([high, low, high, norm_rows(x, -unit(x.shape[0]), 3)], axis=0)


def tile_of(left, right):
    return jnp.exp2(contract_first(left, right))


def folded(tile, row):
    total = tile[:, :128] * row[:, :128]
    for start in range(128, tile.shape[1], 128):
        total = total + tile[:, start:start + 128] * row[:, start:start + 128]
    return total


def as_row(matrix):
    return jnp.sum(matrix.T, axis=0, keepdims=True)


def down(row):
    return jnp.broadcast_to(row, (128, row.shape[1])).T


def wide(column_matrix, columns):
    return jnp.concatenate([column_matrix] * (columns // 128), axis=1)


def owner_of(place, me, devices):
    if devices != GRID_DEVICES:
        return place
    turn, across = ORDER[place // 2]
    return (((me >> 2) - turn + 4) & 3) * 4 + ((me & 3) ^ (2 * across + place % 2))


def prepare_kernel(devices, capacity, *refs):
    (points_in, values_in, mask_in, skeleton_in, top_in, dest_in, leaf_in) = refs[:7]
    piece, to_skel, to_top, lefts, first, last = refs[7:13]
    points, values, mask, skeleton, top, dest, leaf, rights, sems = refs[13:]
    copies = []
    for n, (source, target) in enumerate(zip(refs[:7], (points, values, mask, skeleton, top, dest, leaf))):
        copies.append(pltpu.make_async_copy(source, target, sems.at[n]))
        copies[-1].start()
    for copy in copies:
        copy.wait()
    leaves, features, size = points.shape
    reach = first.shape[0]
    rank = skeleton.shape[1]
    fan_out = dest.shape[0]
    pad = first.shape[1] - features - 1 - reach
    top_total = jnp.zeros((3 * features, rank), F32)
    spot = lax.broadcasted_iota(jnp.int32, (size, rank), 0)
    for l in range(leaves):
        x = points[l]
        chosen = jnp.concatenate(
            [spot == skeleton[l:l + 1, :], spot == top[...] - l * size], axis=1
        )
        picked = jnp.dot(
            jnp.concatenate(thirds(x), axis=0),
            jnp.where(chosen, 1.0, 0.0).astype(BF16),
            preferred_element_type=F32,
        )
        skel = picked[:, :rank]
        skel = skel[:features] + skel[features:2 * features] + skel[2 * features:]
        piece[l * features:(l + 1) * features, :] = skel
        lefts[l] = left_form(skel)
        rights[l] = right_form(x)
        top_total = top_total + picked[:, rank:]
    chosen_top = top_total[:features] + top_total[features:2 * features] + top_total[2 * features:]
    piece[leaves * features:(leaves + 1) * features, :] = chosen_top
    lefts[leaves] = left_form(chosen_top)
    coarse = jnp.zeros((rank, 128), F32)
    base = (leaves + 1) * features
    for l in range(leaves):
        both = tile_of(jnp.concatenate([lefts[l], lefts[leaves]], axis=1), rights[l])
        to_skel[l] = both[:rank]
        to_top[l] = both[rank:]
        row = values[l:l + 1, :]
        piece[base + l:base + l + 1, :] = as_row(folded(both[:rank], row))
        coarse = coarse + folded(both[rank:], row)
    lane = lax.broadcasted_iota(jnp.int32, (1, 128), 1)
    codes = jnp.full((1, 128), -1.0, F32)
    seen = jnp.zeros((1, 128), jnp.int32)
    for l in range(leaves):
        for f in range(fan_out):
            here = lax.div(lane, jnp.int32(capacity)) == dest[f:f + 1, l:l + 1]
            code = (leaf[f:f + 1, l:l + 1] * leaves + l).astype(F32)
            codes = jnp.where(here & (lax.rem(lane, jnp.int32(capacity)) == seen), code, codes)
            seen = seen + here.astype(jnp.int32)
    piece[base + leaves:base + leaves + 8, :] = jnp.concatenate(
        [as_row(coarse), codes, jnp.zeros((6, 128), F32)], axis=0
    )
    for r in range(reach):
        first[r, :features, :] = points[r]
        last[r, :features, :] = points[leaves - reach + r]
        first[r, features:, :] = jnp.broadcast_to(values[r:r + 1, :], (first.shape[1] - features, size))
        own = leaves - reach + r
        rows = [values[own:own + 1, :]]
        rows += [jnp.broadcast_to(mask[s:s + 1, own:own + 1].astype(F32), (1, size)) for s in range(reach)]
        last[r, features:, :] = jnp.concatenate(rows + [jnp.zeros((pad, size), F32)], axis=0)


def edges_of(leaves, reach):
    pairs = [(a, r) for a in range(leaves + reach) for r in range(reach)]
    before = [(a, r) for a, r in pairs if a < reach <= a + 1 + r]
    after = [(a, r) for a, r in pairs if a >= reach and a + 1 + r >= leaves + reach]
    return before, after


def backward(tile, column):
    size = tile.shape[1]
    return jnp.sum((tile * wide(column, size)).reshape(-1, 8, size), axis=0)


def near_kernel(halo, extra, *refs):
    points, values, mask = refs[extra:extra + 3]
    refs = refs[extra + 3:]
    leaves, features, size = points.shape
    if halo:
        following, preceding, out, edges, lefts, rights, downs, across, along = refs
    else:
        out, lefts, rights, downs, across, along = refs
    reach = mask.shape[0]
    before, after = edges_of(leaves, reach)

    def block(e):
        if e < reach:
            return preceding[e, :features, :]
        if e < reach + leaves:
            return points[e - reach]
        return following[e - reach - leaves, :features, :]

    def row_of(e):
        if e < reach:
            return preceding[e, features:features + 1, :]
        if e < reach + leaves:
            return values[e - reach:e - reach + 1, :]
        return following[e - reach - leaves, features:features + 1, :]

    for e in range(leaves + 2 * reach):
        own = reach <= e < leaves + reach
        if own or halo:
            x = block(e)
            if e < leaves + reach:
                lefts[e] = left_form(x)
                downs[e] = down(row_of(e))
            if e >= reach:
                rights[e] = right_form(x)
    for l in range(leaves):
        e = l + reach
        along[l] = backward(tile_of(lefts[e], rights[e]), downs[e])
        across[l] = jnp.zeros((size, 128), F32)
    for a in range(leaves + reach):
        for r in range(reach):
            b = a + 1 + r
            if a >= reach and b < leaves + reach:
                @pl.when(mask[r, a - reach] != 0)
                def _(a=a, b=b):
                    tile = tile_of(lefts[a], rights[b])
                    across[a - reach] += folded(tile, row_of(b))
                    along[b - reach] += backward(tile, downs[a])
    if halo:
        for n, (a, r) in enumerate(before):
            b = a + 1 + r
            tile = tile_of(lefts[a], rights[b]) * preceding[a, features + 1 + r:features + 2 + r, :]
            edges[n] = tile
            along[b - reach] += backward(tile, downs[a])
        for n, (a, r) in enumerate(after):
            b = a + 1 + r
            place = len(before) + n

            @pl.when(mask[r, a - reach] == 0)
            def _(place=place):
                edges[place] = jnp.zeros((size, size), F32)

            @pl.when(mask[r, a - reach] != 0)
            def _(a=a, b=b, place=place):
                tile = tile_of(lefts[a], rights[b])
                edges[place] = tile
                across[a - reach] += folded(tile, row_of(b))

    for l in range(leaves):
        out[l:l + 1, :] = as_row(across[l]) + jnp.sum(along[l], axis=0, keepdims=True)


def far_group(axis, devices, capacity, places, own_piece, pieces, lefts, lists, tiles, tops, sums, scratch):
    targets, vectors, count = lists
    sources, rows, codes, sems = scratch
    leaves = lefts.shape[0] - 1
    features = (pieces[0].shape[0] - 16) // (leaves + 1)
    base = (leaves + 1) * features
    me = lax.axis_index(axis)
    copies = [
        pltpu.make_async_copy(ref.at[base + 8:base + 16, :], codes.at[n], sems.at[n])
        for n, ref in enumerate([own_piece] + list(pieces))
    ]
    for copy in copies:
        copy.start()
    for n, piece in enumerate(pieces):
        tile = tile_of(lefts[leaves], right_form(piece[leaves * features:(leaves + 1) * features, :]))
        tops[n] = tile
        sums[leaves + 1] += tile * piece[base + leaves:base + leaves + 1, :]
    for copy in copies:
        copy.wait()
    filled = 0
    for n, (place, piece) in enumerate(zip(places, pieces)):
        device = owner_of(place, me, devices)
        found = []
        if place == 0 and devices == GRID_DEVICES:
            found += [(l, l, None) for l in range(leaves)]
        for k in range(capacity):
            code = codes[0, 1, device * capacity + k].astype(jnp.int32)
            safe = jnp.maximum(code, 0)
            found.append((lax.rem(safe, leaves), lax.div(safe, leaves), code >= 0))
            code = codes[n + 1, 1, me * capacity + k].astype(jnp.int32)
            safe = jnp.maximum(code, 0)
            found.append((lax.div(safe, leaves), lax.rem(safe, leaves), code >= 0))
        if devices != GRID_DEVICES:
            found += [(l, l, device == me) for l in range(leaves)]
        for target, leaf, used in found:
            start = leaf * features
            if not isinstance(leaf, int):
                start = pl.multiple_of(start, features)
            sources[filled] = piece[pl.ds(start, features), :]
            rows[pl.ds(filled, 1), :] = piece[pl.ds(base + leaf, 1), :]
            targets[filled] = target
            vectors[filled] = device * leaves + leaf
            filled = filled + (1 if used is None else used.astype(jnp.int32))
    count[0] = filled
    for k in range(UNROLL):
        targets[filled + k] = leaves
        vectors[filled + k] = 0
        sources[filled + k] = pieces[0][:features, :]
        rows[pl.ds(filled + k, 1), :] = pieces[0][:1, :]

    def step(g, carry):
        found = []
        for k in range(UNROLL):
            n = g * UNROLL + k
            tile = tile_of(lefts[targets[n]], right_form(sources[n]))
            tiles[n] = tile
            found.append((n, tile * rows[pl.ds(n, 1), :]))
        for n, product in found:
            sums[targets[n]] += product
        return carry

    lax.fori_loop(0, (filled + UNROLL - 1) // UNROLL, step, 0)


def far_rows(sums, to_skel, to_top):
    leaves = to_skel.shape[0]
    mixed = jnp.sum(sums[leaves + 1], axis=1, keepdims=True)
    far, top = [], []
    for l in range(leaves):
        far.append(jnp.sum(to_skel[l] * jnp.sum(sums[l], axis=1, keepdims=True), axis=0, keepdims=True))
        top.append(jnp.sum(to_top[l] * mixed, axis=0, keepdims=True))
    return jnp.concatenate(far, axis=0), jnp.concatenate(top, axis=0)


def total_of(x):
    return jnp.sum(jnp.sum(x, axis=1, keepdims=True), axis=0, keepdims=True)


def in_lanes(*numbers):
    lane = lax.broadcasted_iota(jnp.int32, (1, 128), 1)
    row = jnp.zeros((1, 128), F32)
    for place, number in enumerate(numbers):
        row = jnp.where(lane == place, number, row)
    return row


def early_kernel(extra, axis, devices, capacity, places, *refs):
    refs = refs[extra:]
    n = len(places)
    own_piece, pieces, lefts = refs[0], refs[1:n + 1], refs[n + 1]
    start = None
    if places[0] != 0:
        start, refs = refs[n + 2], refs[:n + 2] + refs[n + 3:]
    targets, vectors, count, tiles, tops, sums = refs[n + 2:n + 8]
    sums[...] = jnp.zeros_like(sums) if start is None else start[...]
    far_group(
        axis, devices, capacity, places, own_piece, pieces, lefts,
        (targets, vectors, count), tiles, tops, sums, refs[n + 8:],
    )


def first_kernel(reach, axis, devices, capacity, places, *refs):
    n = len(places)
    own_piece, pieces, lefts = refs[0], refs[1:n + 1], refs[n + 1]
    so_far, to_skel, to_top, values, near = refs[n + 2:n + 7]
    targets, vectors, count, tiles, tops, image, payload = refs[n + 7:n + 14]
    sums = refs[n + 14]
    sums[...] = so_far[...]
    far_group(
        axis, devices, capacity, places, own_piece, pieces, lefts,
        (targets, vectors, count), tiles, tops, sums, refs[n + 15:],
    )
    leaves, rank, size = to_skel.shape
    far, top = far_rows(sums, to_skel, to_top)
    start = values[...]
    result = start + 0.25 * near[...] + 0.125 * far + 0.25 * top
    image[...] = result
    coarse = jnp.zeros((rank, 128), F32)
    rows = []
    for l in range(leaves):
        row = result[l:l + 1, :]
        rows.append(as_row(folded(to_skel[l], row)))
        coarse = coarse + folded(to_top[l], row)
    rows.append(as_row(coarse))
    rows.append(in_lanes(total_of(start * start), total_of(start * result)))
    rows.append(jnp.zeros((16 - leaves - 2, 128), F32))
    for l in list(range(reach)) + list(range(leaves - reach, leaves)):
        rows += [result[l:l + 1, part:part + 128] for part in range(0, size, 128)]
    payload[...] = jnp.concatenate(rows, axis=0)


def beside_of(me, devices):
    return jnp.where(me == 0, devices - 1, me - 1), jnp.where(me == devices - 1, 0, me + 1)


def second_kernel(reach, axis, devices, groups, *refs):
    lists, refs = refs[:3 * len(groups)], refs[3 * len(groups):]
    tiles, refs = refs[:len(groups)], refs[len(groups):]
    tops, refs = refs[:len(groups)], refs[len(groups):]
    received, refs = refs[:1 if devices != GRID_DEVICES else 4], refs[1 if devices != GRID_DEVICES else 4:]
    to_skel, to_top, values, image, near, edges, residual, along, numbers, everyone, sums, across, beside = refs
    leaves, rank, size = to_skel.shape
    me = lax.axis_index(axis)
    if devices != GRID_DEVICES:
        everyone[...] = received[0][...]
    else:
        for other, blocks in enumerate(received):
            for turn in range(4):
                source = (((me >> 2) - turn + 4) & 3) * 4 + ((me & 3) ^ other)
                everyone[source] = blocks[turn]
    sums[...] = jnp.zeros_like(sums)
    for g, places in enumerate(groups):
        targets, vectors, count = lists[3 * g:3 * g + 3]

        def step(n, carry, g=g, targets=targets, vectors=vectors):
            products = []
            for k in range(UNROLL):
                vector = vectors[n * UNROLL + k]
                products.append(tiles[g][n * UNROLL + k] * everyone[lax.div(vector, leaves), pl.ds(lax.rem(vector, leaves), 1), :])
            for k in range(UNROLL):
                sums[targets[n * UNROLL + k]] += products[k]
            return carry

        lax.fori_loop(0, (count[0] + UNROLL - 1) // UNROLL, step, 0)
        for n, place in enumerate(places):
            device = owner_of(place, me, devices)
            sums[leaves + 1] += tops[g][n] * everyone[device, leaves:leaves + 1, :]
    far, top = far_rows(sums, to_skel, to_top)

    before, after = edges_of(leaves, reach)
    across[...] = jnp.zeros_like(across)
    beside[...] = jnp.zeros_like(beside)

    def edge_row(device, place):
        first = 16 + place * (size // 128)
        return jnp.concatenate([everyone[device, n:n + 1, :] for n in range(first, first + size // 128)], axis=1)

    behind, ahead = beside_of(me, devices)
    for n, (a, r) in enumerate(before):
        beside[a + 1 + r - reach] += backward(edges[n], down(edge_row(behind, reach + a)))
    for n, (a, r) in enumerate(after):
        row = edge_row(ahead, a + 1 + r - reach - leaves)
        across[a - leaves] += folded(edges[len(before) + n], row)
    extra = [jnp.sum(beside[r], axis=0, keepdims=True) for r in range(reach)]
    extra += [jnp.zeros((leaves - 2 * reach, size), F32)]
    extra += [as_row(across[r]) for r in range(reach)]
    start, first = values[...], image[...]
    near_all = near[...] + jnp.concatenate(extra, axis=0)
    second = first + 0.25 * near_all + 0.125 * far + 0.25 * top
    scalars = jnp.sum(everyone[:, leaves + 1, :], axis=0, keepdims=True)
    norm, product = scalars[:, 0:1], scalars[:, 1:2]
    alpha = norm / product
    left = start - alpha * first
    image_left = first - alpha * second
    residual[...] = left
    along[...] = image_left
    row = in_lanes(total_of(left * left), total_of(left * image_left), norm, alpha)
    numbers[...] = jnp.broadcast_to(row, numbers.shape)


def last_kernel(everyone, values, image, residual, along, solution_field, final):
    scalars = jnp.sum(everyone[:, 0, :], axis=0, keepdims=True)
    norm_next, product = scalars[:, 0:1], scalars[:, 1:2]
    norm, alpha = everyone[0, 0:1, 2:3], everyone[0, 0:1, 3:4]
    ratio = norm_next / norm
    step = norm_next / (product - ratio * norm_next / alpha)
    start, left = values[...], residual[...]
    solution_field[...] = alpha * start + step * (left + ratio * start)
    final[...] = left - step * (along[...] + ratio * image[...])


def shape(*dims, dtype=F32):
    return jax.ShapeDtypeStruct(dims, dtype)


SMEM = pl.BlockSpec(memory_space=pltpu.SMEM)
VMEM = pl.BlockSpec(memory_space=pltpu.VMEM)
ANY = pl.BlockSpec(memory_space=pl.ANY)
HBM = pl.BlockSpec(memory_space=pltpu.HBM)


def kernel_call(body, name, inputs, outputs, scratch=(), aliases={}, limit=VMEM_LIMIT, microseconds=1):
    out_specs, out_shapes = zip(*outputs)
    return pl.pallas_call(
        body,
        in_specs=list(inputs),
        out_specs=list(out_specs),
        out_shape=list(out_shapes),
        scratch_shapes=list(scratch),
        input_output_aliases=aliases,
        compiler_params=pltpu.CompilerParams(vmem_limit_bytes=limit),
        cost_estimate=pl.CostEstimate(
            flops=int(microseconds * 1_000_000_000), bytes_accessed=int(microseconds * 3_000_000), transcendentals=0
        ),
        name=name,
    )


def passed_along(block, axis, distance):
    size = lax.axis_size(axis)
    return lax.ppermute(block, axis, [((i - distance) % size, i) for i in range(size)])


def swapped(block, axis, bit):
    return lax.ppermute(block, axis, [(i, i ^ bit) for i in range(lax.axis_size(axis))])


def exchanged(blocks, axis):
    return lax.all_to_all(blocks, axis, split_axis=0, concat_axis=0, tiled=True)


def gathered_blocks(block, axis):
    devices = lax.axis_size(axis)
    if devices != GRID_DEVICES:
        return [exchanged(jnp.broadcast_to(block[None], (devices,) + block.shape), axis)]
    turned = jnp.stack([block] + [passed_along(block, axis, 4 * turn) for turn in (1, 2, 3)])
    return [turned] + [swapped(turned, axis, other) for other in (1, 2, 3)]


def on_device(points, right_side, near_mask, far_dest, far_leaf, skeleton, top_index):
    leaves, features, size = points.shape
    reach = near_mask.shape[1]
    fan_out = far_dest.shape[1]
    rank = skeleton.shape[1]
    devices = lax.axis_size("leaf")
    capacity = max(2, (2 * leaves * fan_out + devices - 1) // devices)
    depth = 3 * features + 16
    piece_rows = (leaves + 1) * features + 16
    halo_rows = features + 8
    integers = jnp.int32
    payload_rows = 16 + 2 * reach * size // rank

    piece, to_skel, to_top, lefts, first, last = kernel_call(
        functools.partial(prepare_kernel, devices, capacity),
        "prepare",
        [HBM] * 7,
        [
            (VMEM, shape(piece_rows, rank)),
            (VMEM, shape(leaves, rank, size)),
            (VMEM, shape(leaves, rank, size)),
            (VMEM, shape(leaves + 1, depth, rank, dtype=BF16)),
            (VMEM, shape(reach, halo_rows, size)),
            (VMEM, shape(reach, halo_rows, size)),
        ],
        [
            pltpu.VMEM(points.shape, F32),
            pltpu.VMEM(right_side.shape, F32),
            pltpu.VMEM(near_mask.T.shape, integers),
            pltpu.VMEM(skeleton.shape, integers),
            pltpu.VMEM(top_index.shape, integers),
            pltpu.VMEM(far_dest.T.shape, integers),
            pltpu.VMEM(far_leaf.T.shape, integers),
            pltpu.VMEM((leaves, depth, size), BF16),
            pltpu.SemaphoreType.DMA((7,)),
        ],
        limit=60 * 1024 * 1024,
        microseconds=2,
    )(points, right_side, near_mask.T, skeleton, top_index, far_dest.T, far_leaf.T)

    following = passed_along(first, "leaf", -1)
    preceding = passed_along(last, "leaf", 1)
    def near_apply(halo, follow, values, *others):
        before, after = edges_of(leaves, reach)
        outputs = [(VMEM, shape(leaves, size))]
        if halo:
            outputs.append((VMEM, shape(len(before) + len(after), size, size)))
        return kernel_call(
            functools.partial(near_kernel, halo, len(follow)),
            "near_first" if halo else "near_second",
            [ANY] * len(follow) + [VMEM, VMEM, SMEM] + [VMEM] * len(others),
            outputs,
            [
                pltpu.VMEM((leaves + reach, depth, size), BF16),
                pltpu.VMEM((leaves + 2 * reach, depth, size), BF16),
                pltpu.VMEM((leaves + reach, size, 128), F32),
                pltpu.VMEM((leaves, size, 128), F32),
                pltpu.VMEM((leaves, 8, size), F32),
            ],
            microseconds=3 if halo else 4,
        )(*follow, points, values, near_mask.T, *others)

    cuts = [devices * cut // GRID_DEVICES for cut in CUTS]
    groups = [tuple(range(start, end)) for start, end in zip(cuts, cuts[1:])]
    if devices == GRID_DEVICES:
        pieces = {}
    else:
        together = lax.all_gather(piece[None], "leaf", axis=0, tiled=True)
        pieces = {place: together[place] for place in range(devices)}
    sums = shape(leaves + 2, rank, rank)

    def group_call(body, name, places, inputs, outputs, scratch, after=()):
        most = -(-(2 * capacity * len(places) + leaves + UNROLL) // UNROLL) * UNROLL
        return kernel_call(
            functools.partial(body, "leaf", devices, capacity, places),
            name,
            [ANY] * (len(after) + 1) + [VMEM] * (len(places) + 1 + len(inputs)),
            [
                (SMEM, shape(most, dtype=integers)),
                (SMEM, shape(most, dtype=integers)),
                (SMEM, shape(1, dtype=integers)),
                (VMEM, shape(most, rank, rank)),
                (VMEM, shape(len(places), rank, rank)),
            ] + outputs,
            scratch + [
                pltpu.VMEM((most, features, rank), F32),
                pltpu.VMEM((most, rank), F32),
                pltpu.SMEM((len(places) + 1, 8, 128), F32),
                pltpu.SemaphoreType.DMA((len(places) + 1,)),
            ],
            microseconds={0: 7, 6: 5, 10: 3}.get(places[0], 3),
        )(*after, piece, *[pieces[place] for place in places], lefts, *inputs)

    def hold(value, *others):
        return lax.optimization_barrier((value, *others))[0]

    def put(slot, value):
        pieces[2 * slot] = value
        pieces[2 * slot + 1] = swapped(value, "leaf", 1)

    passes = []

    def tiles_of_group(*after):
        number = len(passes)
        start = [passes[-1][5]] if passes else []
        passes.append(
            group_call(
                functools.partial(early_kernel, len(after)),
                "far_tiles_%d" % number,
                groups[number],
                start,
                [(VMEM, sums)],
                [],
                after,
            )
        )
        return passes[-1][5]

    if devices == GRID_DEVICES:
        once = passed_along(piece, "leaf", 4)
        twice = passed_along(once, "leaf", 4)
        thrice = passed_along(twice, "leaf", 4)
        near, edges = near_apply(True, (thrice,), right_side, following, preceding)
        put(0, piece)
        put(1, swapped(piece, "leaf", 2))
        put(2, once)
        tiles_of_group(twice)
        put(3, swapped(once, "leaf", 2))
        put(4, twice)
        tiles_of_group(twice)
        put(5, swapped(twice, "leaf", 2))
        put(6, thrice)
        put(7, hold(swapped(thrice, "leaf", 2), tiles_of_group(), near))
    else:
        near, edges = near_apply(True, (), right_side, following, preceding)
        for _ in groups[:-1]:
            tiles_of_group()
    late = group_call(
        functools.partial(first_kernel, reach),
        "far_last",
        groups[3],
        [passes[-1][5], to_skel, to_top, right_side, near],
        [(VMEM, shape(leaves, size)), (VMEM, shape(payload_rows, rank))],
        [pltpu.VMEM(sums.shape, F32)],
    )
    passes.append(late)
    image, payload = late[5:]

    everyone = gathered_blocks(payload, "leaf")
    near_second = near_apply(False, (), image)[0]
    residual, along, numbers = kernel_call(
        functools.partial(second_kernel, reach, "leaf", devices, groups),
        "far_second",
        [SMEM] * (3 * len(groups)) + [VMEM] * (2 * len(groups) + 6 + len(everyone)),
        [
            (VMEM, shape(leaves, size)),
            (VMEM, shape(leaves, size)),
            (VMEM, shape(devices, 1, 128)),
        ],
        [
            pltpu.VMEM((devices, payload_rows, rank), F32),
            pltpu.VMEM(sums.shape, F32),
            pltpu.VMEM((reach, size, 128), F32),
            pltpu.VMEM((reach, 8, size), F32),
        ],
    )(
        *[table for done in passes for table in done[:3]],
        *[done[3] for done in passes],
        *[done[4] for done in passes],
        *everyone, to_skel, to_top, right_side, image, near_second, edges,
    )

    solution_field, final = kernel_call(
        last_kernel,
        "finish",
        [VMEM] * 5,
        [(VMEM, shape(leaves, size)), (VMEM, shape(leaves, size))],
    )(exchanged(numbers, "leaf"), right_side, image, residual, along)
    return solution_field, final


def solution(mesh):
    rows = P(("groups", "leaf"), None)
    in_specs = (P(("groups", "leaf"), None, None),) + (rows,) * 6
    return jax.shard_map(
        on_device, mesh=mesh, in_specs=in_specs, out_specs=(rows, rows), check_vma=False
    )
```

```python
import functools
import math

import jax
import jax.numpy as jnp
from jax import lax
from jax.experimental import pallas as pl
from jax.experimental.pallas import tpu as pltpu
from jax.sharding import PartitionSpec as P

F32 = jnp.float32
BF16 = jnp.bfloat16
VMEM_LIMIT = 20 * 1024 * 1024
UNROLL = 4
GRID_DEVICES = 16
ORDER = ((0, 0), (0, 1), (1, 0), (1, 1), (2, 0), (2, 1), (3, 0), (3, 1))
CUTS = (0, 6, 10, 14, 16)


def contract_first(left, right):
    return lax.dot_general(left, right, (((0,), (0,)), ((), ())), preferred_element_type=F32)


def halves(x):
    high = x.astype(BF16)
    return high, (x - high.astype(F32)).astype(BF16)


def thirds(x):
    high = x.astype(BF16)
    rest = x - high.astype(F32)
    middle = rest.astype(BF16)
    return high, middle, (rest - middle.astype(F32)).astype(BF16)


def norm_rows(x, factor, first):
    norm = jnp.sum(x * x, axis=0, keepdims=True) * factor
    high, middle, low = [piece.astype(F32) for piece in thirds(norm)]
    row = lax.broadcasted_iota(jnp.int32, (16, x.shape[1]), 0)
    rows = jnp.where(row < 6, 1.0, 0.0)
    for place, piece in ((first, high), (first + 1, middle), (first + 2, low)):
        rows = jnp.where(row == place, piece, rows)
    return rows.astype(BF16)


def unit(features):
    return 2.0 / features * math.log2(math.e)


def right_form(x):
    high, low = halves(x)
    return jnp.concatenate([high, high, low, norm_rows(x, -unit(x.shape[0]), 0)], axis=0)


def left_form(x):
    high, low = halves(x * (2.0 * unit(x.shape[0])))
    return jnp.concatenate([high, low, high, norm_rows(x, -unit(x.shape[0]), 3)], axis=0)


def tile_of(left, right):
    return jnp.exp2(contract_first(left, right))


def folded(tile, row):
    total = tile[:, :128] * row[:, :128]
    for start in range(128, tile.shape[1], 128):
        total = total + tile[:, start:start + 128] * row[:, start:start + 128]
    return total


def as_row(matrix):
    return jnp.sum(matrix.T, axis=0, keepdims=True)


def down(row):
    return jnp.broadcast_to(row, (128, row.shape[1])).T


def wide(column_matrix, columns):
    return jnp.concatenate([column_matrix] * (columns // 128), axis=1)


def owner_of(place, me, devices):
    if devices != GRID_DEVICES:
        return place
    turn, across = ORDER[place // 2]
    return (((me >> 2) - turn + 4) & 3) * 4 + ((me & 3) ^ (2 * across + place % 2))


def prepare_kernel(devices, capacity, *refs):
    (points_in, values_in, mask_in, skeleton_in, top_in, dest_in, leaf_in) = refs[:7]
    piece, to_skel, to_top, lefts, first, last = refs[7:13]
    points, values, mask, skeleton, top, dest, leaf, rights, sems = refs[13:]
    copies = []
    for n, (source, target) in enumerate(zip(refs[:7], (points, values, mask, skeleton, top, dest, leaf))):
        copies.append(pltpu.make_async_copy(source, target, sems.at[n]))
        copies[-1].start()
    for copy in copies:
        copy.wait()
    leaves, features, size = points.shape
    reach = first.shape[0]
    rank = skeleton.shape[1]
    fan_out = dest.shape[0]
    pad = first.shape[1] - features - 1 - reach
    top_total = jnp.zeros((3 * features, rank), F32)
    spot = lax.broadcasted_iota(jnp.int32, (size, rank), 0)
    for l in range(leaves):
        x = points[l]
        chosen = jnp.concatenate(
            [spot == skeleton[l:l + 1, :], spot == top[...] - l * size], axis=1
        )
        picked = jnp.dot(
            jnp.concatenate(thirds(x), axis=0),
            jnp.where(chosen, 1.0, 0.0).astype(BF16),
            preferred_element_type=F32,
        )
        skel = picked[:, :rank]
        skel = skel[:features] + skel[features:2 * features] + skel[2 * features:]
        piece[l * features:(l + 1) * features, :] = skel
        lefts[l] = left_form(skel)
        rights[l] = right_form(x)
        top_total = top_total + picked[:, rank:]
    chosen_top = top_total[:features] + top_total[features:2 * features] + top_total[2 * features:]
    piece[leaves * features:(leaves + 1) * features, :] = chosen_top
    lefts[leaves] = left_form(chosen_top)
    coarse = jnp.zeros((rank, 128), F32)
    base = (leaves + 1) * features
    for l in range(leaves):
        both = tile_of(jnp.concatenate([lefts[l], lefts[leaves]], axis=1), rights[l])
        to_skel[l] = both[:rank]
        to_top[l] = both[rank:]
        row = values[l:l + 1, :]
        piece[base + l:base + l + 1, :] = as_row(folded(both[:rank], row))
        coarse = coarse + folded(both[rank:], row)
    lane = lax.broadcasted_iota(jnp.int32, (1, 128), 1)
    codes = jnp.full((1, 128), -1.0, F32)
    seen = jnp.zeros((1, 128), jnp.int32)
    for l in range(leaves):
        for f in range(fan_out):
            here = lax.div(lane, jnp.int32(capacity)) == dest[f:f + 1, l:l + 1]
            code = (leaf[f:f + 1, l:l + 1] * leaves + l).astype(F32)
            codes = jnp.where(here & (lax.rem(lane, jnp.int32(capacity)) == seen), code, codes)
            seen = seen + here.astype(jnp.int32)
    piece[base + leaves:base + leaves + 8, :] = jnp.concatenate(
        [as_row(coarse), codes, jnp.zeros((6, 128), F32)], axis=0
    )
    for r in range(reach):
        first[r, :features, :] = points[r]
        last[r, :features, :] = points[leaves - reach + r]
        first[r, features:, :] = jnp.broadcast_to(values[r:r + 1, :], (first.shape[1] - features, size))
        own = leaves - reach + r
        rows = [values[own:own + 1, :]]
        rows += [jnp.broadcast_to(mask[s:s + 1, own:own + 1].astype(F32), (1, size)) for s in range(reach)]
        last[r, features:, :] = jnp.concatenate(rows + [jnp.zeros((pad, size), F32)], axis=0)


def edges_of(leaves, reach):
    pairs = [(a, r) for a in range(leaves + reach) for r in range(reach)]
    before = [(a, r) for a, r in pairs if a < reach <= a + 1 + r]
    after = [(a, r) for a, r in pairs if a >= reach and a + 1 + r >= leaves + reach]
    return before, after


def backward(tile, column):
    size = tile.shape[1]
    return jnp.sum((tile * wide(column, size)).reshape(-1, 8, size), axis=0)


def near_kernel(halo, extra, *refs):
    points, values, mask = refs[extra:extra + 3]
    refs = refs[extra + 3:]
    leaves, features, size = points.shape
    if halo:
        following, preceding, out, edges, lefts, rights, downs, across, along = refs
    else:
        out, lefts, rights, downs, across, along = refs
    reach = mask.shape[0]
    before, after = edges_of(leaves, reach)

    def block(e):
        if e < reach:
            return preceding[e, :features, :]
        if e < reach + leaves:
            return points[e - reach]
        return following[e - reach - leaves, :features, :]

    def row_of(e):
        if e < reach:
            return preceding[e, features:features + 1, :]
        if e < reach + leaves:
            return values[e - reach:e - reach + 1, :]
        return following[e - reach - leaves, features:features + 1, :]

    for e in range(leaves + 2 * reach):
        own = reach <= e < leaves + reach
        if own or halo:
            x = block(e)
            if e < leaves + reach:
                lefts[e] = left_form(x)
                downs[e] = down(row_of(e))
            if e >= reach:
                rights[e] = right_form(x)
    for l in range(leaves):
        e = l + reach
        along[l] = backward(tile_of(lefts[e], rights[e]), downs[e])
        across[l] = jnp.zeros((size, 128), F32)
    for a in range(leaves + reach):
        for r in range(reach):
            b = a + 1 + r
            if a >= reach and b < leaves + reach:
                @pl.when(mask[r, a - reach] != 0)
                def _(a=a, b=b):
                    tile = tile_of(lefts[a], rights[b])
                    across[a - reach] += folded(tile, row_of(b))
                    along[b - reach] += backward(tile, downs[a])
    if halo:
        for n, (a, r) in enumerate(before):
            b = a + 1 + r
            tile = tile_of(lefts[a], rights[b]) * preceding[a, features + 1 + r:features + 2 + r, :]
            edges[n] = tile
            along[b - reach] += backward(tile, downs[a])
        for n, (a, r) in enumerate(after):
            b = a + 1 + r
            place = len(before) + n

            @pl.when(mask[r, a - reach] == 0)
            def _(place=place):
                edges[place] = jnp.zeros((size, size), F32)

            @pl.when(mask[r, a - reach] != 0)
            def _(a=a, b=b, place=place):
                tile = tile_of(lefts[a], rights[b])
                edges[place] = tile
                across[a - reach] += folded(tile, row_of(b))

    for l in range(leaves):
        out[l:l + 1, :] = as_row(across[l]) + jnp.sum(along[l], axis=0, keepdims=True)


def far_group(axis, devices, capacity, places, own_piece, pieces, lefts, lists, tiles, tops, sums, scratch):
    targets, vectors, count = lists
    sources, rows, codes, sems = scratch
    leaves = lefts.shape[0] - 1
    features = (pieces[0].shape[0] - 16) // (leaves + 1)
    base = (leaves + 1) * features
    me = lax.axis_index(axis)
    copies = [
        pltpu.make_async_copy(ref.at[base + 8:base + 16, :], codes.at[n], sems.at[n])
        for n, ref in enumerate([own_piece] + list(pieces))
    ]
    for copy in copies:
        copy.start()
    for n, piece in enumerate(pieces):
        tile = tile_of(lefts[leaves], right_form(piece[leaves * features:(leaves + 1) * features, :]))
        tops[n] = tile
        sums[leaves + 1] += tile * piece[base + leaves:base + leaves + 1, :]
    for copy in copies:
        copy.wait()
    filled = 0
    for n, (place, piece) in enumerate(zip(places, pieces)):
        device = owner_of(place, me, devices)
        found = []
        if place == 0 and devices == GRID_DEVICES:
            found += [(l, l, None) for l in range(leaves)]
        for k in range(capacity):
            code = codes[0, 1, device * capacity + k].astype(jnp.int32)
            safe = jnp.maximum(code, 0)
            found.append((lax.rem(safe, leaves), lax.div(safe, leaves), code >= 0))
            code = codes[n + 1, 1, me * capacity + k].astype(jnp.int32)
            safe = jnp.maximum(code, 0)
            found.append((lax.div(safe, leaves), lax.rem(safe, leaves), code >= 0))
        if devices != GRID_DEVICES:
            found += [(l, l, device == me) for l in range(leaves)]
        for target, leaf, used in found:
            start = leaf * features
            if not isinstance(leaf, int):
                start = pl.multiple_of(start, features)
            sources[filled] = piece[pl.ds(start, features), :]
            rows[pl.ds(filled, 1), :] = piece[pl.ds(base + leaf, 1), :]
            targets[filled] = target
            vectors[filled] = device * leaves + leaf
            filled = filled + (1 if used is None else used.astype(jnp.int32))
    count[0] = filled
    for k in range(UNROLL):
        targets[filled + k] = leaves
        vectors[filled + k] = 0
        sources[filled + k] = pieces[0][:features, :]
        rows[pl.ds(filled + k, 1), :] = pieces[0][:1, :]

    def step(g, carry):
        found = []
        for k in range(UNROLL):
            n = g * UNROLL + k
            tile = tile_of(lefts[targets[n]], right_form(sources[n]))
            tiles[n] = tile
            found.append((n, tile * rows[pl.ds(n, 1), :]))
        for n, product in found:
            sums[targets[n]] += product
        return carry

    lax.fori_loop(0, (filled + UNROLL - 1) // UNROLL, step, 0)


def far_rows(sums, to_skel, to_top):
    leaves = to_skel.shape[0]
    mixed = jnp.sum(sums[leaves + 1], axis=1, keepdims=True)
    far, top = [], []
    for l in range(leaves):
        far.append(jnp.sum(to_skel[l] * jnp.sum(sums[l], axis=1, keepdims=True), axis=0, keepdims=True))
        top.append(jnp.sum(to_top[l] * mixed, axis=0, keepdims=True))
    return jnp.concatenate(far, axis=0), jnp.concatenate(top, axis=0)


def total_of(x):
    return jnp.sum(jnp.sum(x, axis=1, keepdims=True), axis=0, keepdims=True)


def in_lanes(*numbers):
    lane = lax.broadcasted_iota(jnp.int32, (1, 128), 1)
    row = jnp.zeros((1, 128), F32)
    for place, number in enumerate(numbers):
        row = jnp.where(lane == place, number, row)
    return row


def early_kernel(extra, axis, devices, capacity, places, *refs):
    refs = refs[extra:]
    n = len(places)
    own_piece, pieces, lefts = refs[0], refs[1:n + 1], refs[n + 1]
    start = None
    if places[0] != 0:
        start, refs = refs[n + 2], refs[:n + 2] + refs[n + 3:]
    targets, vectors, count, tiles, tops, sums = refs[n + 2:n + 8]
    sums[...] = jnp.zeros_like(sums) if start is None else start[...]
    far_group(
        axis, devices, capacity, places, own_piece, pieces, lefts,
        (targets, vectors, count), tiles, tops, sums, refs[n + 8:],
    )


def first_kernel(reach, axis, devices, capacity, places, *refs):
    n = len(places)
    own_piece, pieces, lefts = refs[0], refs[1:n + 1], refs[n + 1]
    so_far, to_skel, to_top, values, near = refs[n + 2:n + 7]
    targets, vectors, count, tiles, tops, image, payload = refs[n + 7:n + 14]
    sums = refs[n + 14]
    sums[...] = so_far[...]
    far_group(
        axis, devices, capacity, places, own_piece, pieces, lefts,
        (targets, vectors, count), tiles, tops, sums, refs[n + 15:],
    )
    leaves, rank, size = to_skel.shape
    far, top = far_rows(sums, to_skel, to_top)
    start = values[...]
    result = start + 0.25 * near[...] + 0.125 * far + 0.25 * top
    image[...] = result
    coarse = jnp.zeros((rank, 128), F32)
    rows = []
    for l in range(leaves):
        row = result[l:l + 1, :]
        rows.append(as_row(folded(to_skel[l], row)))
        coarse = coarse + folded(to_top[l], row)
    rows.append(as_row(coarse))
    rows.append(in_lanes(total_of(start * start), total_of(start * result)))
    rows.append(jnp.zeros((16 - leaves - 2, 128), F32))
    for l in list(range(reach)) + list(range(leaves - reach, leaves)):
        rows += [result[l:l + 1, part:part + 128] for part in range(0, size, 128)]
    payload[...] = jnp.concatenate(rows, axis=0)


def beside_of(me, devices):
    return jnp.where(me == 0, devices - 1, me - 1), jnp.where(me == devices - 1, 0, me + 1)


def second_kernel(reach, axis, devices, groups, *refs):
    lists, refs = refs[:3 * len(groups)], refs[3 * len(groups):]
    tiles, refs = refs[:len(groups)], refs[len(groups):]
    tops, refs = refs[:len(groups)], refs[len(groups):]
    received, refs = refs[:1 if devices != GRID_DEVICES else 4], refs[1 if devices != GRID_DEVICES else 4:]
    to_skel, to_top, values, image, near, edges, residual, along, numbers, everyone, sums, across, beside = refs
    leaves, rank, size = to_skel.shape
    me = lax.axis_index(axis)
    if devices != GRID_DEVICES:
        everyone[...] = received[0][...]
    else:
        for other, blocks in enumerate(received):
            for turn in range(4):
                source = (((me >> 2) - turn + 4) & 3) * 4 + ((me & 3) ^ other)
                everyone[source] = blocks[turn]
    sums[...] = jnp.zeros_like(sums)
    for g, places in enumerate(groups):
        targets, vectors, count = lists[3 * g:3 * g + 3]

        def step(n, carry, g=g, targets=targets, vectors=vectors):
            products = []
            for k in range(UNROLL):
                vector = vectors[n * UNROLL + k]
                products.append(tiles[g][n * UNROLL + k] * everyone[lax.div(vector, leaves), pl.ds(lax.rem(vector, leaves), 1), :])
            for k in range(UNROLL):
                sums[targets[n * UNROLL + k]] += products[k]
            return carry

        lax.fori_loop(0, (count[0] + UNROLL - 1) // UNROLL, step, 0)
        for n, place in enumerate(places):
            device = owner_of(place, me, devices)
            sums[leaves + 1] += tops[g][n] * everyone[device, leaves:leaves + 1, :]
    far, top = far_rows(sums, to_skel, to_top)

    before, after = edges_of(leaves, reach)
    across[...] = jnp.zeros_like(across)
    beside[...] = jnp.zeros_like(beside)

    def edge_row(device, place):
        first = 16 + place * (size // 128)
        return jnp.concatenate([everyone[device, n:n + 1, :] for n in range(first, first + size // 128)], axis=1)

    behind, ahead = beside_of(me, devices)
    for n, (a, r) in enumerate(before):
        beside[a + 1 + r - reach] += backward(edges[n], down(edge_row(behind, reach + a)))
    for n, (a, r) in enumerate(after):
        row = edge_row(ahead, a + 1 + r - reach - leaves)
        across[a - leaves] += folded(edges[len(before) + n], row)
    extra = [jnp.sum(beside[r], axis=0, keepdims=True) for r in range(reach)]
    extra += [jnp.zeros((leaves - 2 * reach, size), F32)]
    extra += [as_row(across[r]) for r in range(reach)]
    start, first = values[...], image[...]
    near_all = near[...] + jnp.concatenate(extra, axis=0)
    second = first + 0.25 * near_all + 0.125 * far + 0.25 * top
    scalars = jnp.sum(everyone[:, leaves + 1, :], axis=0, keepdims=True)
    norm, product = scalars[:, 0:1], scalars[:, 1:2]
    alpha = norm / product
    left = start - alpha * first
    image_left = first - alpha * second
    residual[...] = left
    along[...] = image_left
    row = in_lanes(total_of(left * left), total_of(left * image_left), norm, alpha)
    numbers[...] = jnp.broadcast_to(row, numbers.shape)


def last_kernel(everyone, values, image, residual, along, solution_field, final):
    scalars = jnp.sum(everyone[:, 0, :], axis=0, keepdims=True)
    norm_next, product = scalars[:, 0:1], scalars[:, 1:2]
    norm, alpha = everyone[0, 0:1, 2:3], everyone[0, 0:1, 3:4]
    ratio = norm_next / norm
    step = norm_next / (product - ratio * norm_next / alpha)
    start, left = values[...], residual[...]
    solution_field[...] = alpha * start + step * (left + ratio * start)
    final[...] = left - step * (along[...] + ratio * image[...])


def shape(*dims, dtype=F32):
    return jax.ShapeDtypeStruct(dims, dtype)


SMEM = pl.BlockSpec(memory_space=pltpu.SMEM)
VMEM = pl.BlockSpec(memory_space=pltpu.VMEM)
ANY = pl.BlockSpec(memory_space=pl.ANY)
HBM = pl.BlockSpec(memory_space=pltpu.HBM)


def kernel_call(body, name, inputs, outputs, scratch=(), aliases={}, limit=VMEM_LIMIT, microseconds=1):
    out_specs, out_shapes = zip(*outputs)
    return pl.pallas_call(
        body,
        in_specs=list(inputs),
        out_specs=list(out_specs),
        out_shape=list(out_shapes),
        scratch_shapes=list(scratch),
        input_output_aliases=aliases,
        compiler_params=pltpu.CompilerParams(vmem_limit_bytes=limit),
        cost_estimate=pl.CostEstimate(
            flops=int(microseconds * 1_000_000_000), bytes_accessed=int(microseconds * 3_000_000), transcendentals=0
        ),
        name=name,
    )


def passed_along(block, axis, distance):
    size = lax.axis_size(axis)
    return lax.ppermute(block, axis, [((i - distance) % size, i) for i in range(size)])


def swapped(block, axis, bit):
    return lax.ppermute(block, axis, [(i, i ^ bit) for i in range(lax.axis_size(axis))])


def exchanged(blocks, axis):
    return lax.all_to_all(blocks, axis, split_axis=0, concat_axis=0, tiled=True)


def gathered_blocks(block, axis):
    devices = lax.axis_size(axis)
    if devices != GRID_DEVICES:
        return [exchanged(jnp.broadcast_to(block[None], (devices,) + block.shape), axis)]
    turned = jnp.stack([block] + [passed_along(block, axis, 4 * turn) for turn in (1, 2, 3)])
    return [turned] + [swapped(turned, axis, other) for other in (1, 2, 3)]


def on_device(points, right_side, near_mask, far_dest, far_leaf, skeleton, top_index):
    leaves, features, size = points.shape
    reach = near_mask.shape[1]
    fan_out = far_dest.shape[1]
    rank = skeleton.shape[1]
    devices = lax.axis_size("leaf")
    capacity = max(2, (2 * leaves * fan_out + devices - 1) // devices)
    depth = 3 * features + 16
    piece_rows = (leaves + 1) * features + 16
    halo_rows = features + 8
    integers = jnp.int32
    payload_rows = 16 + 2 * reach * size // rank

    piece, to_skel, to_top, lefts, first, last = kernel_call(
        functools.partial(prepare_kernel, devices, capacity),
        "prepare",
        [HBM] * 7,
        [
            (VMEM, shape(piece_rows, rank)),
            (VMEM, shape(leaves, rank, size)),
            (VMEM, shape(leaves, rank, size)),
            (VMEM, shape(leaves + 1, depth, rank, dtype=BF16)),
            (VMEM, shape(reach, halo_rows, size)),
            (VMEM, shape(reach, halo_rows, size)),
        ],
        [
            pltpu.VMEM(points.shape, F32),
            pltpu.VMEM(right_side.shape, F32),
            pltpu.VMEM(near_mask.T.shape, integers),
            pltpu.VMEM(skeleton.shape, integers),
            pltpu.VMEM(top_index.shape, integers),
            pltpu.VMEM(far_dest.T.shape, integers),
            pltpu.VMEM(far_leaf.T.shape, integers),
            pltpu.VMEM((leaves, depth, size), BF16),
            pltpu.SemaphoreType.DMA((7,)),
        ],
        limit=60 * 1024 * 1024,
        microseconds=2,
    )(points, right_side, near_mask.T, skeleton, top_index, far_dest.T, far_leaf.T)

    following = passed_along(first, "leaf", -1)
    preceding = passed_along(last, "leaf", 1)
    def near_apply(halo, follow, values, *others):
        before, after = edges_of(leaves, reach)
        outputs = [(VMEM, shape(leaves, size))]
        if halo:
            outputs.append((VMEM, shape(len(before) + len(after), size, size)))
        return kernel_call(
            functools.partial(near_kernel, halo, len(follow)),
            "near_first" if halo else "near_second",
            [ANY] * len(follow) + [VMEM, VMEM, SMEM] + [VMEM] * len(others),
            outputs,
            [
                pltpu.VMEM((leaves + reach, depth, size), BF16),
                pltpu.VMEM((leaves + 2 * reach, depth, size), BF16),
                pltpu.VMEM((leaves + reach, size, 128), F32),
                pltpu.VMEM((leaves, size, 128), F32),
                pltpu.VMEM((leaves, 8, size), F32),
            ],
            microseconds=3 if halo else 4,
        )(*follow, points, values, near_mask.T, *others)

    cuts = [devices * cut // GRID_DEVICES for cut in CUTS]
    groups = [tuple(range(start, end)) for start, end in zip(cuts, cuts[1:])]
    if devices == GRID_DEVICES:
        pieces = {}
    else:
        together = lax.all_gather(piece[None], "leaf", axis=0, tiled=True)
        pieces = {place: together[place] for place in range(devices)}
    sums = shape(leaves + 2, rank, rank)

    def group_call(body, name, places, inputs, outputs, scratch, after=()):
        most = -(-(2 * capacity * len(places) + leaves + UNROLL) // UNROLL) * UNROLL
        return kernel_call(
            functools.partial(body, "leaf", devices, capacity, places),
            name,
            [ANY] * (len(after) + 1) + [VMEM] * (len(places) + 1 + len(inputs)),
            [
                (SMEM, shape(most, dtype=integers)),
                (SMEM, shape(most, dtype=integers)),
                (SMEM, shape(1, dtype=integers)),
                (VMEM, shape(most, rank, rank)),
                (VMEM, shape(len(places), rank, rank)),
            ] + outputs,
            scratch + [
                pltpu.VMEM((most, features, rank), F32),
                pltpu.VMEM((most, rank), F32),
                pltpu.SMEM((len(places) + 1, 8, 128), F32),
                pltpu.SemaphoreType.DMA((len(places) + 1,)),
            ],
            microseconds={0: 9, 6: 5, 10: 3}.get(places[0], 3),
        )(*after, piece, *[pieces[place] for place in places], lefts, *inputs)

    def hold(value, *others):
        return lax.optimization_barrier((value, *others))[0]

    def put(slot, value):
        pieces[2 * slot] = value
        pieces[2 * slot + 1] = swapped(value, "leaf", 1)

    passes = []

    def tiles_of_group(*after):
        number = len(passes)
        start = [passes[-1][5]] if passes else []
        passes.append(
            group_call(
                functools.partial(early_kernel, len(after)),
                "far_tiles_%d" % number,
                groups[number],
                start,
                [(VMEM, sums)],
                [],
                after,
            )
        )
        return passes[-1][5]

    if devices == GRID_DEVICES:
        once = passed_along(piece, "leaf", 4)
        twice = passed_along(once, "leaf", 4)
        thrice = passed_along(twice, "leaf", 4)
        near, edges = near_apply(True, (once,), right_side, following, preceding)
        put(0, piece)
        put(1, swapped(piece, "leaf", 2))
        put(2, once)
        tiles_of_group(twice)
        put(3, swapped(once, "leaf", 2))
        put(4, twice)
        tiles_of_group(twice)
        put(5, swapped(twice, "leaf", 2))
        put(6, thrice)
        put(7, hold(swapped(thrice, "leaf", 2), tiles_of_group(), near))
    else:
        near, edges = near_apply(True, (), right_side, following, preceding)
        for _ in groups[:-1]:
            tiles_of_group()
    late = group_call(
        functools.partial(first_kernel, reach),
        "far_last",
        groups[3],
        [passes[-1][5], to_skel, to_top, right_side, near],
        [(VMEM, shape(leaves, size)), (VMEM, shape(payload_rows, rank))],
        [pltpu.VMEM(sums.shape, F32)],
    )
    passes.append(late)
    image, payload = late[5:]

    everyone = gathered_blocks(payload, "leaf")
    near_second = near_apply(False, (), image)[0]
    residual, along, numbers = kernel_call(
        functools.partial(second_kernel, reach, "leaf", devices, groups),
        "far_second",
        [SMEM] * (3 * len(groups)) + [VMEM] * (2 * len(groups) + 6 + len(everyone)),
        [
            (VMEM, shape(leaves, size)),
            (VMEM, shape(leaves, size)),
            (VMEM, shape(devices, 1, 128)),
        ],
        [
            pltpu.VMEM((devices, payload_rows, rank), F32),
            pltpu.VMEM(sums.shape, F32),
            pltpu.VMEM((reach, size, 128), F32),
            pltpu.VMEM((reach, 8, size), F32),
        ],
    )(
        *[table for done in passes for table in done[:3]],
        *[done[3] for done in passes],
        *[done[4] for done in passes],
        *everyone, to_skel, to_top, right_side, image, near_second, edges,
    )

    solution_field, final = kernel_call(
        last_kernel,
        "finish",
        [VMEM] * 5,
        [(VMEM, shape(leaves, size)), (VMEM, shape(leaves, size))],
    )(exchanged(numbers, "leaf"), right_side, image, residual, along)
    return solution_field, final


def solution(mesh):
    rows = P(("groups", "leaf"), None)
    in_specs = (P(("groups", "leaf"), None, None),) + (rows,) * 6
    return jax.shard_map(
        on_device, mesh=mesh, in_specs=in_specs, out_specs=(rows, rows), check_vma=False
    )
```

```python
import functools
import math

import jax
import jax.numpy as jnp
from jax import lax
from jax.experimental import pallas as pl
from jax.experimental.pallas import tpu as pltpu
from jax.sharding import PartitionSpec as P

F32 = jnp.float32
BF16 = jnp.bfloat16
VMEM_LIMIT = 20 * 1024 * 1024
UNROLL = 4
PARTS = 4
GRID_DEVICES = 16
ORDER = ((0, 0), (0, 1), (1, 0), (1, 1), (2, 0), (2, 1), (3, 0), (3, 1))
CUTS = (0, 6, 10, 14, 16)


def contract_first(left, right):
    return lax.dot_general(left, right, (((0,), (0,)), ((), ())), preferred_element_type=F32)


def halves(x):
    high = x.astype(BF16)
    return high, (x - high.astype(F32)).astype(BF16)


def thirds(x):
    high = x.astype(BF16)
    rest = x - high.astype(F32)
    middle = rest.astype(BF16)
    return high, middle, (rest - middle.astype(F32)).astype(BF16)


def norm_rows(x, factor, first):
    norm = jnp.sum(x * x, axis=0, keepdims=True) * factor
    high, middle, low = [piece.astype(F32) for piece in thirds(norm)]
    row = lax.broadcasted_iota(jnp.int32, (16, x.shape[1]), 0)
    rows = jnp.where(row < 6, 1.0, 0.0)
    for place, piece in ((first, high), (first + 1, middle), (first + 2, low)):
        rows = jnp.where(row == place, piece, rows)
    return rows.astype(BF16)


def unit(features):
    return 2.0 / features * math.log2(math.e)


def right_form(x):
    high, low = halves(x)
    return jnp.concatenate([high, high, low, norm_rows(x, -unit(x.shape[0]), 0)], axis=0)


def left_form(x):
    high, low = halves(x * (2.0 * unit(x.shape[0])))
    return jnp.concatenate([high, low, high, norm_rows(x, -unit(x.shape[0]), 3)], axis=0)


def tile_of(left, right):
    return jnp.exp2(contract_first(left, right))


def folded(tile, row):
    total = tile[:, :128] * row[:, :128]
    for start in range(128, tile.shape[1], 128):
        total = total + tile[:, start:start + 128] * row[:, start:start + 128]
    return total


def as_row(matrix):
    return jnp.sum(matrix.T, axis=0, keepdims=True)


def down(row):
    return jnp.broadcast_to(row, (128, row.shape[1])).T


def wide(column_matrix, columns):
    return jnp.concatenate([column_matrix] * (columns // 128), axis=1)


def owner_of(place, me, devices):
    if devices != GRID_DEVICES:
        return place
    turn, across = ORDER[place // 2]
    return (((me >> 2) - turn + 4) & 3) * 4 + ((me & 3) ^ (2 * across + place % 2))


def prepare_kernel(devices, capacity, *refs):
    (points_in, values_in, mask_in, skeleton_in, top_in, dest_in, leaf_in) = refs[:7]
    piece, to_skel, to_top, lefts, first, last = refs[7:13]
    points, values, mask, skeleton, top, dest, leaf, rights, sems = refs[13:]
    copies = []
    for n, (source, target) in enumerate(zip(refs[:7], (points, values, mask, skeleton, top, dest, leaf))):
        copies.append(pltpu.make_async_copy(source, target, sems.at[n]))
        copies[-1].start()
    for copy in copies:
        copy.wait()
    leaves, features, size = points.shape
    reach = first.shape[0]
    rank = skeleton.shape[1]
    fan_out = dest.shape[0]
    pad = first.shape[1] - features - 1 - reach
    top_total = jnp.zeros((3 * features, rank), F32)
    spot = lax.broadcasted_iota(jnp.int32, (size, rank), 0)
    for l in range(leaves):
        x = points[l]
        chosen = jnp.concatenate(
            [spot == skeleton[l:l + 1, :], spot == top[...] - l * size], axis=1
        )
        picked = jnp.dot(
            jnp.concatenate(thirds(x), axis=0),
            jnp.where(chosen, 1.0, 0.0).astype(BF16),
            preferred_element_type=F32,
        )
        skel = picked[:, :rank]
        skel = skel[:features] + skel[features:2 * features] + skel[2 * features:]
        piece[l * features:(l + 1) * features, :] = skel
        lefts[l] = left_form(skel)
        rights[l] = right_form(x)
        top_total = top_total + picked[:, rank:]
    chosen_top = top_total[:features] + top_total[features:2 * features] + top_total[2 * features:]
    piece[leaves * features:(leaves + 1) * features, :] = chosen_top
    lefts[leaves] = left_form(chosen_top)
    coarse = jnp.zeros((rank, 128), F32)
    base = (leaves + 1) * features
    for l in range(leaves):
        both = tile_of(jnp.concatenate([lefts[l], lefts[leaves]], axis=1), rights[l])
        to_skel[l] = both[:rank]
        to_top[l] = both[rank:]
        row = values[l:l + 1, :]
        piece[base + l:base + l + 1, :] = as_row(folded(both[:rank], row))
        coarse = coarse + folded(both[rank:], row)
    lane = lax.broadcasted_iota(jnp.int32, (1, 128), 1)
    codes = jnp.full((1, 128), -1.0, F32)
    seen = jnp.zeros((1, 128), jnp.int32)
    for l in range(leaves):
        for f in range(fan_out):
            here = lax.div(lane, jnp.int32(capacity)) == dest[f:f + 1, l:l + 1]
            code = (leaf[f:f + 1, l:l + 1] * leaves + l).astype(F32)
            codes = jnp.where(here & (lax.rem(lane, jnp.int32(capacity)) == seen), code, codes)
            seen = seen + here.astype(jnp.int32)
    piece[base + leaves:base + leaves + 8, :] = jnp.concatenate(
        [as_row(coarse), codes, jnp.zeros((6, 128), F32)], axis=0
    )
    for r in range(reach):
        first[r, :features, :] = points[r]
        last[r, :features, :] = points[leaves - reach + r]
        first[r, features:, :] = jnp.broadcast_to(values[r:r + 1, :], (first.shape[1] - features, size))
        own = leaves - reach + r
        rows = [values[own:own + 1, :]]
        rows += [jnp.broadcast_to(mask[s:s + 1, own:own + 1].astype(F32), (1, size)) for s in range(reach)]
        last[r, features:, :] = jnp.concatenate(rows + [jnp.zeros((pad, size), F32)], axis=0)


def edges_of(leaves, reach):
    pairs = [(a, r) for a in range(leaves + reach) for r in range(reach)]
    before = [(a, r) for a, r in pairs if a < reach <= a + 1 + r]
    after = [(a, r) for a, r in pairs if a >= reach and a + 1 + r >= leaves + reach]
    return before, after


def backward(tile, column):
    size = tile.shape[1]
    return jnp.sum((tile * wide(column, size)).reshape(-1, 8, size), axis=0)


def near_kernel(halo, extra, *refs):
    points, values, mask = refs[extra:extra + 3]
    refs = refs[extra + 3:]
    leaves, features, size = points.shape
    if halo:
        following, preceding, out, edges, lefts, rights, downs, across, along = refs
    else:
        out, lefts, rights, downs, across, along = refs
    reach = mask.shape[0]
    before, after = edges_of(leaves, reach)

    def block(e):
        if e < reach:
            return preceding[e, :features, :]
        if e < reach + leaves:
            return points[e - reach]
        return following[e - reach - leaves, :features, :]

    def row_of(e):
        if e < reach:
            return preceding[e, features:features + 1, :]
        if e < reach + leaves:
            return values[e - reach:e - reach + 1, :]
        return following[e - reach - leaves, features:features + 1, :]

    for e in range(leaves + 2 * reach):
        own = reach <= e < leaves + reach
        if own or halo:
            x = block(e)
            if e < leaves + reach:
                lefts[e] = left_form(x)
                downs[e] = down(row_of(e))
            if e >= reach:
                rights[e] = right_form(x)
    for l in range(leaves):
        e = l + reach
        along[l] = backward(tile_of(lefts[e], rights[e]), downs[e])
        across[l] = jnp.zeros((size, 128), F32)
    for a in range(leaves + reach):
        for r in range(reach):
            b = a + 1 + r
            if a >= reach and b < leaves + reach:
                @pl.when(mask[r, a - reach] != 0)
                def _(a=a, b=b):
                    tile = tile_of(lefts[a], rights[b])
                    across[a - reach] += folded(tile, row_of(b))
                    along[b - reach] += backward(tile, downs[a])
    if halo:
        for n, (a, r) in enumerate(before):
            b = a + 1 + r
            tile = tile_of(lefts[a], rights[b]) * preceding[a, features + 1 + r:features + 2 + r, :]
            edges[n] = tile
            along[b - reach] += backward(tile, downs[a])
        for n, (a, r) in enumerate(after):
            b = a + 1 + r
            place = len(before) + n

            @pl.when(mask[r, a - reach] == 0)
            def _(place=place):
                edges[place] = jnp.zeros((size, size), F32)

            @pl.when(mask[r, a - reach] != 0)
            def _(a=a, b=b, place=place):
                tile = tile_of(lefts[a], rights[b])
                edges[place] = tile
                across[a - reach] += folded(tile, row_of(b))

    for l in range(leaves):
        out[l:l + 1, :] = as_row(across[l]) + jnp.sum(along[l], axis=0, keepdims=True)


def far_group(axis, devices, capacity, places, own_piece, pieces, lefts, lists, tiles, tops, sums, scratch):
    targets, vectors, count = lists
    sources, rows, codes, sems = scratch
    leaves = lefts.shape[0] - 1
    features = (pieces[0].shape[0] - 16) // (leaves + 1)
    base = (leaves + 1) * features
    me = lax.axis_index(axis)
    copies = [
        pltpu.make_async_copy(ref.at[base + 8:base + 16, :], codes.at[n], sems.at[n])
        for n, ref in enumerate([own_piece] + list(pieces))
    ]
    for copy in copies:
        copy.start()
    for n, piece in enumerate(pieces):
        tile = tile_of(lefts[leaves], right_form(piece[leaves * features:(leaves + 1) * features, :]))
        tops[n] = tile
        sums[leaves + 1] += tile * piece[base + leaves:base + leaves + 1, :]
    for copy in copies:
        copy.wait()
    filled = 0
    for n, (place, piece) in enumerate(zip(places, pieces)):
        device = owner_of(place, me, devices)
        found = []
        if place == 0 and devices == GRID_DEVICES:
            found += [(l, l, None) for l in range(leaves)]
        for k in range(capacity):
            code = codes[0, 1, device * capacity + k].astype(jnp.int32)
            safe = jnp.maximum(code, 0)
            found.append((lax.rem(safe, leaves), lax.div(safe, leaves), code >= 0))
            code = codes[n + 1, 1, me * capacity + k].astype(jnp.int32)
            safe = jnp.maximum(code, 0)
            found.append((lax.div(safe, leaves), lax.rem(safe, leaves), code >= 0))
        if devices != GRID_DEVICES:
            found += [(l, l, device == me) for l in range(leaves)]
        for target, leaf, used in found:
            start = leaf * features
            if not isinstance(leaf, int):
                start = pl.multiple_of(start, features)
            sources[filled] = piece[pl.ds(start, features), :]
            rows[pl.ds(filled, 1), :] = piece[pl.ds(base + leaf, 1), :]
            targets[filled] = target
            vectors[filled] = device * leaves + leaf
            filled = filled + (1 if used is None else used.astype(jnp.int32))
    count[0] = filled
    for k in range(UNROLL):
        targets[filled + k] = leaves
        vectors[filled + k] = 0
        sources[filled + k] = pieces[0][:features, :]
        rows[pl.ds(filled + k, 1), :] = pieces[0][:1, :]

    def step(g, carry):
        found = []
        for k in range(UNROLL):
            n = g * UNROLL + k
            tile = tile_of(lefts[targets[n]], right_form(sources[n]))
            tiles[n] = tile
            found.append((n, tile * rows[pl.ds(n, 1), :]))
        for n, product in found:
            sums[targets[n]] += product
        return carry

    lax.fori_loop(0, (filled + UNROLL - 1) // UNROLL, step, 0)


def far_rows(sum_of, mixed, to_skel, to_top):
    leaves = to_skel.shape[0]
    mixed = jnp.sum(mixed, axis=1, keepdims=True)
    far, top = [], []
    for l in range(leaves):
        far.append(jnp.sum(to_skel[l] * jnp.sum(sum_of(l), axis=1, keepdims=True), axis=0, keepdims=True))
        top.append(jnp.sum(to_top[l] * mixed, axis=0, keepdims=True))
    return jnp.concatenate(far, axis=0), jnp.concatenate(top, axis=0)


def total_of(x):
    return jnp.sum(jnp.sum(x, axis=1, keepdims=True), axis=0, keepdims=True)


def in_lanes(*numbers):
    lane = lax.broadcasted_iota(jnp.int32, (1, 128), 1)
    row = jnp.zeros((1, 128), F32)
    for place, number in enumerate(numbers):
        row = jnp.where(lane == place, number, row)
    return row


def early_kernel(extra, axis, devices, capacity, places, *refs):
    refs = refs[extra:]
    n = len(places)
    own_piece, pieces, lefts = refs[0], refs[1:n + 1], refs[n + 1]
    start = None
    if places[0] != 0:
        start, refs = refs[n + 2], refs[:n + 2] + refs[n + 3:]
    targets, vectors, count, tiles, tops, sums = refs[n + 2:n + 8]
    sums[...] = jnp.zeros_like(sums) if start is None else start[...]
    far_group(
        axis, devices, capacity, places, own_piece, pieces, lefts,
        (targets, vectors, count), tiles, tops, sums, refs[n + 8:],
    )


def first_kernel(reach, axis, devices, capacity, places, *refs):
    n = len(places)
    own_piece, pieces, lefts = refs[0], refs[1:n + 1], refs[n + 1]
    so_far, to_skel, to_top, values, near = refs[n + 2:n + 7]
    targets, vectors, count, tiles, tops, image, payload = refs[n + 7:n + 14]
    sums = refs[n + 14]
    sums[...] = so_far[...]
    far_group(
        axis, devices, capacity, places, own_piece, pieces, lefts,
        (targets, vectors, count), tiles, tops, sums, refs[n + 15:],
    )
    leaves, rank, size = to_skel.shape
    far, top = far_rows(lambda l: sums[l], sums[leaves + 1], to_skel, to_top)
    start = values[...]
    result = start + 0.25 * near[...] + 0.125 * far + 0.25 * top
    image[...] = result
    coarse = jnp.zeros((rank, 128), F32)
    rows = []
    for l in range(leaves):
        row = result[l:l + 1, :]
        rows.append(as_row(folded(to_skel[l], row)))
        coarse = coarse + folded(to_top[l], row)
    rows.append(as_row(coarse))
    rows.append(in_lanes(total_of(start * start), total_of(start * result)))
    rows.append(jnp.zeros((16 - leaves - 2, 128), F32))
    for l in list(range(reach)) + list(range(leaves - reach, leaves)):
        rows += [result[l:l + 1, part:part + 128] for part in range(0, size, 128)]
    payload[...] = jnp.concatenate(rows, axis=0)


def beside_of(me, devices):
    return jnp.where(me == 0, devices - 1, me - 1), jnp.where(me == devices - 1, 0, me + 1)


def second_kernel(reach, axis, devices, groups, *refs):
    lists, refs = refs[:3 * len(groups)], refs[3 * len(groups):]
    tiles, refs = refs[:len(groups)], refs[len(groups):]
    tops, refs = refs[:len(groups)], refs[len(groups):]
    received, refs = refs[:1 if devices != GRID_DEVICES else 4], refs[1 if devices != GRID_DEVICES else 4:]
    to_skel, to_top, values, image, near, edges, residual, along, numbers, everyone, *sums, across, beside = refs
    leaves, rank, size = to_skel.shape
    me = lax.axis_index(axis)
    if devices != GRID_DEVICES:
        everyone[...] = received[0][...]
    else:
        for other, blocks in enumerate(received):
            for turn in range(4):
                source = (((me >> 2) - turn + 4) & 3) * 4 + ((me & 3) ^ other)
                everyone[source] = blocks[turn]
    for part in sums:
        part[...] = jnp.zeros_like(part)
    mixed = jnp.zeros((rank, rank), F32)
    for g, places in enumerate(groups):
        targets, vectors, count = lists[3 * g:3 * g + 3]

        def step(n, carry, g=g, targets=targets, vectors=vectors):
            products = []
            for k in range(UNROLL):
                vector = vectors[n * UNROLL + k]
                products.append(tiles[g][n * UNROLL + k] * everyone[lax.div(vector, leaves), pl.ds(lax.rem(vector, leaves), 1), :])
            for k in range(UNROLL):
                sums[k % len(sums)][targets[n * UNROLL + k]] += products[k]
            return carry

        lax.fori_loop(0, (count[0] + UNROLL - 1) // UNROLL, step, 0)
        for n, place in enumerate(places):
            device = owner_of(place, me, devices)
            mixed = mixed + tops[g][n] * everyone[device, leaves:leaves + 1, :]
    far, top = far_rows(lambda l: sum(part[l] for part in sums), mixed, to_skel, to_top)

    before, after = edges_of(leaves, reach)
    across[...] = jnp.zeros_like(across)
    beside[...] = jnp.zeros_like(beside)

    def edge_row(device, place):
        first = 16 + place * (size // 128)
        return jnp.concatenate([everyone[device, n:n + 1, :] for n in range(first, first + size // 128)], axis=1)

    behind, ahead = beside_of(me, devices)
    for n, (a, r) in enumerate(before):
        beside[a + 1 + r - reach] += backward(edges[n], down(edge_row(behind, reach + a)))
    for n, (a, r) in enumerate(after):
        row = edge_row(ahead, a + 1 + r - reach - leaves)
        across[a - leaves] += folded(edges[len(before) + n], row)
    extra = [jnp.sum(beside[r], axis=0, keepdims=True) for r in range(reach)]
    extra += [jnp.zeros((leaves - 2 * reach, size), F32)]
    extra += [as_row(across[r]) for r in range(reach)]
    start, first = values[...], image[...]
    near_all = near[...] + jnp.concatenate(extra, axis=0)
    second = first + 0.25 * near_all + 0.125 * far + 0.25 * top
    scalars = jnp.sum(everyone[:, leaves + 1, :], axis=0, keepdims=True)
    norm, product = scalars[:, 0:1], scalars[:, 1:2]
    alpha = norm / product
    left = start - alpha * first
    image_left = first - alpha * second
    residual[...] = left
    along[...] = image_left
    row = in_lanes(total_of(left * left), total_of(left * image_left), norm, alpha)
    numbers[...] = jnp.broadcast_to(row, numbers.shape)


def last_kernel(everyone, values, image, residual, along, solution_field, final):
    scalars = jnp.sum(everyone[:, 0, :], axis=0, keepdims=True)
    norm_next, product = scalars[:, 0:1], scalars[:, 1:2]
    norm, alpha = everyone[0, 0:1, 2:3], everyone[0, 0:1, 3:4]
    ratio = norm_next / norm
    step = norm_next / (product - ratio * norm_next / alpha)
    start, left = values[...], residual[...]
    solution_field[...] = alpha * start + step * (left + ratio * start)
    final[...] = left - step * (along[...] + ratio * image[...])


def shape(*dims, dtype=F32):
    return jax.ShapeDtypeStruct(dims, dtype)


SMEM = pl.BlockSpec(memory_space=pltpu.SMEM)
VMEM = pl.BlockSpec(memory_space=pltpu.VMEM)
ANY = pl.BlockSpec(memory_space=pl.ANY)
HBM = pl.BlockSpec(memory_space=pltpu.HBM)


def kernel_call(body, name, inputs, outputs, scratch=(), aliases={}, limit=VMEM_LIMIT, microseconds=1):
    out_specs, out_shapes = zip(*outputs)
    return pl.pallas_call(
        body,
        in_specs=list(inputs),
        out_specs=list(out_specs),
        out_shape=list(out_shapes),
        scratch_shapes=list(scratch),
        input_output_aliases=aliases,
        compiler_params=pltpu.CompilerParams(vmem_limit_bytes=limit),
        cost_estimate=pl.CostEstimate(
            flops=int(microseconds * 1_000_000_000), bytes_accessed=int(microseconds * 3_000_000), transcendentals=0
        ),
        name=name,
    )


def passed_along(block, axis, distance):
    size = lax.axis_size(axis)
    return lax.ppermute(block, axis, [((i - distance) % size, i) for i in range(size)])


def swapped(block, axis, bit):
    return lax.ppermute(block, axis, [(i, i ^ bit) for i in range(lax.axis_size(axis))])


def exchanged(blocks, axis):
    return lax.all_to_all(blocks, axis, split_axis=0, concat_axis=0, tiled=True)


def gathered_blocks(block, axis):
    devices = lax.axis_size(axis)
    if devices != GRID_DEVICES:
        return [exchanged(jnp.broadcast_to(block[None], (devices,) + block.shape), axis)]
    turned = jnp.stack([block] + [passed_along(block, axis, 4 * turn) for turn in (1, 2, 3)])
    return [turned] + [swapped(turned, axis, other) for other in (1, 2, 3)]


def on_device(points, right_side, near_mask, far_dest, far_leaf, skeleton, top_index):
    leaves, features, size = points.shape
    reach = near_mask.shape[1]
    fan_out = far_dest.shape[1]
    rank = skeleton.shape[1]
    devices = lax.axis_size("leaf")
    capacity = max(2, (2 * leaves * fan_out + devices - 1) // devices)
    depth = 3 * features + 16
    piece_rows = (leaves + 1) * features + 16
    halo_rows = features + 8
    integers = jnp.int32
    payload_rows = 16 + 2 * reach * size // rank

    piece, to_skel, to_top, lefts, first, last = kernel_call(
        functools.partial(prepare_kernel, devices, capacity),
        "prepare",
        [HBM] * 7,
        [
            (VMEM, shape(piece_rows, rank)),
            (VMEM, shape(leaves, rank, size)),
            (VMEM, shape(leaves, rank, size)),
            (VMEM, shape(leaves + 1, depth, rank, dtype=BF16)),
            (VMEM, shape(reach, halo_rows, size)),
            (VMEM, shape(reach, halo_rows, size)),
        ],
        [
            pltpu.VMEM(points.shape, F32),
            pltpu.VMEM(right_side.shape, F32),
            pltpu.VMEM(near_mask.T.shape, integers),
            pltpu.VMEM(skeleton.shape, integers),
            pltpu.VMEM(top_index.shape, integers),
            pltpu.VMEM(far_dest.T.shape, integers),
            pltpu.VMEM(far_leaf.T.shape, integers),
            pltpu.VMEM((leaves, depth, size), BF16),
            pltpu.SemaphoreType.DMA((7,)),
        ],
        limit=60 * 1024 * 1024,
        microseconds=2,
    )(points, right_side, near_mask.T, skeleton, top_index, far_dest.T, far_leaf.T)

    following = passed_along(first, "leaf", -1)
    preceding = passed_along(last, "leaf", 1)
    def near_apply(halo, follow, values, *others):
        before, after = edges_of(leaves, reach)
        outputs = [(VMEM, shape(leaves, size))]
        if halo:
            outputs.append((VMEM, shape(len(before) + len(after), size, size)))
        return kernel_call(
            functools.partial(near_kernel, halo, len(follow)),
            "near_first" if halo else "near_second",
            [ANY] * len(follow) + [VMEM, VMEM, SMEM] + [VMEM] * len(others),
            outputs,
            [
                pltpu.VMEM((leaves + reach, depth, size), BF16),
                pltpu.VMEM((leaves + 2 * reach, depth, size), BF16),
                pltpu.VMEM((leaves + reach, size, 128), F32),
                pltpu.VMEM((leaves, size, 128), F32),
                pltpu.VMEM((leaves, 8, size), F32),
            ],
            microseconds=3 if halo else 4,
        )(*follow, points, values, near_mask.T, *others)

    cuts = [devices * cut // GRID_DEVICES for cut in CUTS]
    groups = [tuple(range(start, end)) for start, end in zip(cuts, cuts[1:])]
    if devices == GRID_DEVICES:
        pieces = {}
    else:
        together = lax.all_gather(piece[None], "leaf", axis=0, tiled=True)
        pieces = {place: together[place] for place in range(devices)}
    sums = shape(leaves + 2, rank, rank)

    def group_call(body, name, places, inputs, outputs, scratch, after=()):
        most = -(-(2 * capacity * len(places) + leaves + UNROLL) // UNROLL) * UNROLL
        return kernel_call(
            functools.partial(body, "leaf", devices, capacity, places),
            name,
            [ANY] * (len(after) + 1) + [VMEM] * (len(places) + 1 + len(inputs)),
            [
                (SMEM, shape(most, dtype=integers)),
                (SMEM, shape(most, dtype=integers)),
                (SMEM, shape(1, dtype=integers)),
                (VMEM, shape(most, rank, rank)),
                (VMEM, shape(len(places), rank, rank)),
            ] + outputs,
            scratch + [
                pltpu.VMEM((most, features, rank), F32),
                pltpu.VMEM((most, rank), F32),
                pltpu.SMEM((len(places) + 1, 8, 128), F32),
                pltpu.SemaphoreType.DMA((len(places) + 1,)),
            ],
            microseconds={0: 9, 6: 5, 10: 3}.get(places[0], 3),
        )(*after, piece, *[pieces[place] for place in places], lefts, *inputs)

    def hold(value, *others):
        return lax.optimization_barrier((value, *others))[0]

    def put(slot, value):
        pieces[2 * slot] = value
        pieces[2 * slot + 1] = swapped(value, "leaf", 1)

    passes = []

    def tiles_of_group(*after):
        number = len(passes)
        start = [passes[-1][5]] if passes else []
        passes.append(
            group_call(
                functools.partial(early_kernel, len(after)),
                "far_tiles_%d" % number,
                groups[number],
                start,
                [(VMEM, sums)],
                [],
                after,
            )
        )
        return passes[-1][5]

    if devices == GRID_DEVICES:
        once = passed_along(piece, "leaf", 4)
        twice = passed_along(once, "leaf", 4)
        thrice = passed_along(twice, "leaf", 4)
        near, edges = near_apply(True, (once,), right_side, following, preceding)
        put(0, piece)
        put(1, swapped(piece, "leaf", 2))
        put(2, once)
        tiles_of_group(twice)
        put(3, swapped(once, "leaf", 2))
        put(4, twice)
        tiles_of_group(twice)
        put(5, swapped(twice, "leaf", 2))
        put(6, thrice)
        put(7, hold(swapped(thrice, "leaf", 2), tiles_of_group(), near))
    else:
        near, edges = near_apply(True, (), right_side, following, preceding)
        for _ in groups[:-1]:
            tiles_of_group()
    late = group_call(
        functools.partial(first_kernel, reach),
        "far_last",
        groups[3],
        [passes[-1][5], to_skel, to_top, right_side, near],
        [(VMEM, shape(leaves, size)), (VMEM, shape(payload_rows, rank))],
        [pltpu.VMEM(sums.shape, F32)],
    )
    passes.append(late)
    image, payload = late[5:]

    everyone = gathered_blocks(payload, "leaf")
    near_second = near_apply(False, (), image)[0]
    residual, along, numbers = kernel_call(
        functools.partial(second_kernel, reach, "leaf", devices, groups),
        "far_second",
        [SMEM] * (3 * len(groups)) + [VMEM] * (2 * len(groups) + 6 + len(everyone)),
        [
            (VMEM, shape(leaves, size)),
            (VMEM, shape(leaves, size)),
            (VMEM, shape(devices, 1, 128)),
        ],
        [
            pltpu.VMEM((devices, payload_rows, rank), F32),
        ]
        + [pltpu.VMEM((leaves + 1, rank, rank), F32)] * PARTS
        + [
            pltpu.VMEM((reach, size, 128), F32),
            pltpu.VMEM((reach, 8, size), F32),
        ],
    )(
        *[table for done in passes for table in done[:3]],
        *[done[3] for done in passes],
        *[done[4] for done in passes],
        *everyone, to_skel, to_top, right_side, image, near_second, edges,
    )

    solution_field, final = kernel_call(
        last_kernel,
        "finish",
        [VMEM] * 5,
        [(VMEM, shape(leaves, size)), (VMEM, shape(leaves, size))],
    )(exchanged(numbers, "leaf"), right_side, image, residual, along)
    return solution_field, final


def solution(mesh):
    rows = P(("groups", "leaf"), None)
    in_specs = (P(("groups", "leaf"), None, None),) + (rows,) * 6
    return jax.shard_map(
        on_device, mesh=mesh, in_specs=in_specs, out_specs=(rows, rows), check_vma=False
    )
```
